32 devices in a mesh: row: 8 (over z, core), col: 4 (over y, x).
Axes of the slice: x: 2, y: 2, z: 4, core: 2. Of those that a mesh axis runs over, the one named last changes fastest.
Arguments:
- rhs: float32 [16, 64, 128], P('col'), may hold values from -6 to 6
- diag_inv: float32 [16, 128, 128], P('col'), as said below
- panel: bfloat16 [16, 16, 128, 128], P('row', 'col'), may hold values from -0.09375 to 0.09375
- offdiag: bfloat16 [512, 16, 128, 128], P('row', 'col'), may hold values from -0.0234375 to 0.0234375
- known: bfloat16 [64, 64, 128], P(('row', 'col')), may hold values from -6 to 6
- row_index: int32 [512], P('row'), may hold values from 0 to 7
Outputs:
- solution: bfloat16 [16, 64, 128], P('col')
The draws below stay inside these ranges and needn't reach their ends.
Inputs may be any that keep to these rules, and one draw needn't show every extreme that they name: Each block of diag_inv is lower triangular (the inverse of a lower triangular diagonal block).
All inputs are finite; a program needn't handle non-finite values.
Results may differ from the reference program's by a relative error of at most 0.015.
Values may be sent and summed in bfloat16 or wider, within the bound.
No kernel may reach another device: no remote copies, remote signals or barrier semaphores. Data moves between devices by JAX's collectives and lax.ppermute only.
A program may use at most 64 MiB of HBM per device.

```python
import jax
import jax.numpy as jnp
import numpy as np
from jax import lax

NB = 16
BS = 128
RHS = 64
OFF_DEV = 64
NOFF = 512
K_ROW = 8
NK = 64
N_ROW = 8
N_COL = 4


def draw_diag_inv(key, part):
    first, second = jax.random.split(jax.random.fold_in(key, 17))
    lower = jnp.arange(BS)[:, None] > jnp.arange(BS)[None, :]
    eye = jnp.arange(BS)[:, None] == jnp.arange(BS)[None, :]
    spread = 0.5 * jax.random.normal(first, (NB, BS, BS), jnp.float32) / jnp.sqrt(jnp.float32(BS))
    diag = jax.random.uniform(second, (NB, BS, BS), jnp.float32, 0.6, 1.4)
    return jnp.where(lower[None], spread, 0.0) + jnp.where(eye[None], diag, 0.0)


def with_ends(values, own_key, low, top_value):
    spot = [jax.random.randint(jax.random.fold_in(own_key, axis), (), 0, length) for axis, length in enumerate(values.shape)]
    widest = values.shape.index(max(values.shape))
    beside = spot[:widest] + [(spot[widest] + 1) % values.shape[widest]] + spot[widest + 1:]
    return values.at[tuple(spot)].set(low).at[tuple(beside)].set(top_value)


def steps_of(own_key, shape, pieces, least, top_value):
    loudness = 1.0
    for axis_at, blocks in pieces:
        heights = jax.random.uniform(jax.random.fold_in(jax.random.fold_in(own_key, 6), axis_at), (blocks,), jnp.float32, least / len(pieces), top_value / len(pieces))
        loudness = loudness * jnp.repeat(jnp.exp(heights), shape[axis_at] // blocks).reshape((-1,) + (1,) * (len(shape) - 1 - axis_at))
    return loudness


def centred(stream_key, dims, width, limit, shards=(), dtype=jnp.bfloat16):
    values = jax.random.normal(stream_key, dims, jnp.float32) * width
    if len(shards) > 0:
        values = steps_of(stream_key, dims, shards, -0.22, 0.18) * values
    return jnp.clip(values, min=-limit, max=limit).astype(dtype)


def setup_inputs(seed: int = 0) -> dict:
    keys = jax.random.split(jax.random.key(seed), 7)
    rhs = centred(keys[0], (NB, RHS, BS), 1.0, 6.0, ((0, 4),), jnp.float32)
    diag_inv = draw_diag_inv(jax.random.fold_in(keys[6], 71), 0)
    panel = centred(keys[2], (NB, NB, BS, BS), (2 * NB * BS) ** -0.5, 0.09375, ((0, 8), (1, 4)))
    offdiag = centred(keys[3], (NOFF, NB, BS, BS), (NOFF * BS) ** -0.5, 0.0234375, ((0, 8), (1, 4)))
    known = centred(keys[4], (NK, RHS, BS), 1.0, 6.0, ((0, 32),))
    row_index = with_ends(jax.random.randint(keys[5], (NOFF,), 0, K_ROW), jax.random.fold_in(keys[5], 1), 0, K_ROW - 1).astype(jnp.int32)
    return dict(rhs=rhs, diag_inv=diag_inv, panel=panel, offdiag=offdiag, known=known, row_index=row_index)


def positions(count, parts):
    return np.array([(k % parts) * (count // parts) + k // parts for k in range(count)])


def reference(rhs, diag_inv, panel, offdiag, known, row_index):
    col_pos = positions(NB, N_COL)
    row_pos = positions(NB, N_ROW)
    owner_base = jnp.asarray((np.arange(NOFF) // OFF_DEV) * K_ROW).astype(jnp.int32)
    picked = known[owner_base + row_index.astype(jnp.int32)].astype(jnp.float32)

    def one_column(stored):
        tiles = lax.dynamic_index_in_dim(offdiag, stored, 1, keepdims=False).astype(jnp.float32)
        return jnp.einsum('pqi,pia->qa', picked, tiles)

    off_sum = lax.map(one_column, jnp.asarray(col_pos).astype(jnp.int32))
    update = rhs[col_pos] - off_sum
    solved = [None] * NB
    for k in reversed(range(NB)):
        total = update[k]
        for j in range(k + 1, NB):
            total = total - jnp.dot(solved[j], panel[row_pos[j], col_pos[k]], preferred_element_type=jnp.float32)
        solved[k] = jnp.dot(total, diag_inv[col_pos[k]], precision=lax.Precision.HIGHEST, preferred_element_type=jnp.float32).astype(jnp.bfloat16)
    slots = NB // N_COL
    order = [(s % slots) * N_COL + s // slots for s in range(NB)]
    return jnp.stack([solved[k] for k in order])
```

```python
import functools

import jax
import jax.numpy as jnp
from jax import lax
from jax.experimental import pallas as pl
from jax.experimental.pallas import tpu as pltpu
from jax.sharding import PartitionSpec as P

NB = 16
AXES = ("row", "col")
VMEM_LIMIT = 48 * 1024 * 1024
HIGHEST = lax.Precision.HIGHEST


def tile_slots(rows, cols):
    return [
        (a, b)
        for a in reversed(range(NB // rows))
        for b in reversed(range(NB // cols))
        if a * rows + rows - 1 > b * cols
    ]


def send(array, rows, cols, target):
    pairs = []
    for r in range(rows):
        for c in range(cols):
            to_r, to_c = target(r, c)
            pairs.append((r * cols + c, to_r * cols + to_c))
    return lax.ppermute(array, AXES, pairs)


def along_z(array, rows, cols, step):
    return send(array, rows, cols, lambda r, c: ((r + 2 * step) % rows, c))


def along_col(array, rows, cols, step):
    return send(array, rows, cols, lambda r, c: (r, (c + step) % cols))


def other_core(array, rows, cols):
    return send(array, rows, cols, lambda r, c: (r ^ 1, c))


def fold_kernel(slots, panel_ref, inverse_ref, out_ref):
    for at, (a, b) in enumerate(slots):
        inverse = inverse_ref[b]
        high = inverse.astype(jnp.bfloat16)
        low = (inverse - high.astype(jnp.float32)).astype(jnp.bfloat16)
        tile = panel_ref[a, b]
        out_ref[at] = (
            jnp.dot(tile, high, preferred_element_type=jnp.float32)
            + jnp.dot(tile, low, preferred_element_type=jnp.float32)
        ).astype(jnp.bfloat16)


def fold_panel(panel, inverse, slots):
    bs = panel.shape[-1]
    return pl.pallas_call(
        functools.partial(fold_kernel, slots),
        out_shape=jax.ShapeDtypeStruct((len(slots), bs, bs), jnp.bfloat16),
        compiler_params=pltpu.CompilerParams(vmem_limit_bytes=VMEM_LIMIT),
        name="fold_panel",
    )(panel, inverse)


def segment_kernel(chunk, index_ref, tiles_ref, out_ref, sums):
    step = pl.program_id(0)
    blocks, bs = tiles_ref.shape[1], tiles_ref.shape[2]

    @pl.when(step == 0)
    def _():
        sums[...] = jnp.zeros_like(sums)

    for p in range(chunk):
        segment = index_ref[step * chunk + p]
        for b in range(blocks):
            cols = slice(b * bs, (b + 1) * bs)
            sums[segment, :, cols] += tiles_ref[p, b].astype(jnp.float32)

    @pl.when(step == pl.num_programs(0) - 1)
    def _():
        out_ref[...] = sums[...].astype(jnp.bfloat16)


def segment_sums(offdiag, row_index, segments):
    tiles, blocks, bs, _ = offdiag.shape
    chunk = 8
    return pl.pallas_call(
        functools.partial(segment_kernel, chunk),
        grid_spec=pltpu.PrefetchScalarGridSpec(
            num_scalar_prefetch=1,
            grid=(tiles // chunk,),
            in_specs=[pl.BlockSpec((chunk, blocks, bs, bs), lambda i, index: (i, 0, 0, 0))],
            out_specs=pl.BlockSpec((segments, bs, blocks * bs), lambda i, index: (0, 0, 0)),
            scratch_shapes=[pltpu.VMEM((segments, bs, blocks * bs), jnp.float32)],
        ),
        out_shape=jax.ShapeDtypeStruct((segments, bs, blocks * bs), jnp.bfloat16),
        compiler_params=pltpu.CompilerParams(vmem_limit_bytes=VMEM_LIMIT),
        cost_estimate=pl.CostEstimate(
            flops=offdiag.size, bytes_accessed=2 * offdiag.size, transcendentals=0
        ),
        name="segment_sums",
    )(row_index, offdiag)


def update_kernel(cols, *refs):
    known_refs, (sums_ref, rhs_ref, inverse_ref, keep_ref, give_ref, whole) = refs[:cols], refs[cols:]
    blocks, count, bs = rhs_ref.shape
    per = known_refs[0].shape[0]
    row_id, col_id = lax.axis_index("row"), lax.axis_index("col")
    off = jnp.zeros((count, blocks * bs), jnp.float32)
    for step in range(cols):
        first = lax.rem(col_id + cols - step, cols) * per
        for i in range(per):
            off += jnp.dot(
                known_refs[step][i], sums_ref[first + i], preferred_element_type=jnp.float32
            )
    adds = (row_id == 0).astype(jnp.float32)
    for b in range(blocks):
        total = rhs_ref[b] * adds - off[:, b * bs : (b + 1) * bs]
        whole[b] = jnp.dot(
            total, inverse_ref[b], precision=HIGHEST, preferred_element_type=jnp.float32
        )
    half = count // 2
    core = lax.rem(row_id, 2)
    keep = pl.ds(pl.multiple_of(core * half, half), half)
    give = pl.ds(pl.multiple_of((1 - core) * half, half), half)
    keep_ref[...] = whole[:, keep, :]
    give_ref[...] = whole[:, give, :].astype(jnp.bfloat16)


def local_update(known, sums, rhs, inverse):
    blocks, count, bs = rhs.shape
    half = (blocks, count // 2, bs)
    return pl.pallas_call(
        functools.partial(update_kernel, len(known)),
        out_shape=(
            jax.ShapeDtypeStruct(half, jnp.float32),
            jax.ShapeDtypeStruct(half, jnp.bfloat16),
        ),
        scratch_shapes=[pltpu.VMEM(rhs.shape, jnp.float32)],
        compiler_params=pltpu.CompilerParams(vmem_limit_bytes=VMEM_LIMIT),
        name="local_update",
    )(*known, sums, rhs, inverse)


def chain_kernel(rows, cols, slots, *refs):
    zs = rows // 2
    value_refs, refs = refs[:cols], refs[cols:]
    piece_refs, refs = (refs[:cols], refs[cols : 2 * cols]), refs[2 * cols :]
    out_ref, tiles, values, solved, sems = refs
    row_id, col_id = lax.axis_index("row"), lax.axis_index("col")
    core, z = lax.rem(row_id, 2), row_id // 2
    copies = []
    for side in range(2):
        for step in range(cols):
            owner_col = lax.rem(col_id + cols - step, cols)
            for back in range(zs):
                owner_z = lax.rem(z + zs - back, zs)
                owner_core = core if side == 0 else 1 - core
                copy = pltpu.make_async_copy(
                    piece_refs[side][step].at[back],
                    tiles.at[2 * owner_z + owner_core, owner_col],
                    sems.at[len(copies)],
                )
                copy.start()
                copies.append(copy)
    per = value_refs[0].shape[0]
    for step in range(cols):
        owner_col = lax.rem(col_id + cols - step, cols)
        for b in range(per):
            values[b * cols + owner_col] = value_refs[step][b].astype(jnp.float32)
    for copy in copies:
        copy.wait()
    sums = [values[k] for k in range(NB)]
    for j in reversed(range(NB)):
        block = sums[j].astype(jnp.bfloat16)
        solved[j] = block
        for k in reversed(range(j)):
            at = slots.index((j // rows, k // cols))
            sums[k] = sums[k] - jnp.dot(
                block, tiles[j % rows, k % cols, at], preferred_element_type=jnp.float32
            )
    for b in range(per):
        out_ref[b] = solved[b * cols + col_id]


def chain(values, own, other, rows, cols, slots):
    per, half, bs = values[0].shape
    anywhere = pl.BlockSpec(memory_space=pl.ANY)
    vmem = pl.BlockSpec(memory_space=pltpu.VMEM)
    return pl.pallas_call(
        functools.partial(chain_kernel, rows, cols, slots),
        in_specs=[vmem] * cols + [anywhere] * (2 * cols),
        out_specs=vmem,
        out_shape=jax.ShapeDtypeStruct((per, half, bs), jnp.bfloat16),
        scratch_shapes=[
            pltpu.VMEM((rows, cols, len(slots), bs, bs), jnp.bfloat16),
            pltpu.VMEM((NB, half, bs), jnp.float32),
            pltpu.VMEM((NB, half, bs), jnp.bfloat16),
            pltpu.SemaphoreType.DMA((rows * cols,)),
        ],
        compiler_params=pltpu.CompilerParams(vmem_limit_bytes=VMEM_LIMIT),
        name="chain",
    )(*values, *own, *other)


def body(rhs, diag_inv, panel, offdiag, known, row_index):
    rows, cols = lax.axis_size("row"), lax.axis_size("col")
    zs = rows // 2
    slots = tile_slots(rows, cols)

    known_all = [known] + [along_col(known, rows, cols, d) for d in range(1, cols)]
    folded = fold_panel(panel, diag_inv, slots)
    line = jnp.stack([folded] + [along_z(folded, rows, cols, d) for d in range(1, zs)])
    own = [line] + [along_col(line, rows, cols, d) for d in range(1, cols)]
    other = [other_core(piece, rows, cols) for piece in own]

    sums = segment_sums(offdiag, row_index, known.shape[0] * cols)
    keep, give = local_update(known_all, sums, rhs, diag_inv)
    part = (keep + other_core(give, rows, cols).astype(jnp.float32)).astype(jnp.bfloat16)
    total = part.astype(jnp.float32)
    for d in range(1, zs):
        total = total + along_z(part, rows, cols, d).astype(jnp.float32)
    total = total.astype(jnp.bfloat16)
    values = [total] + [along_col(total, rows, cols, d) for d in range(1, cols)]

    mine = chain(values, own, other, rows, cols, slots)
    theirs = other_core(mine, rows, cols)
    first = lax.rem(lax.axis_index("row"), 2) == 0
    return jnp.concatenate(
        [jnp.where(first, mine, theirs), jnp.where(first, theirs, mine)], axis=1
    )


def solution(mesh):
    placed = (
        P("col", None, None),
        P("col", None, None),
        P("row", "col", None, None),
        P("row", "col", None, None),
        P(("row", "col"), None, None),
        P("row"),
    )
    return jax.shard_map(
        body, mesh=mesh, in_specs=placed, out_specs=P("col", None, None), check_vma=False
    )
```

```python
import functools

import jax
import jax.numpy as jnp
from jax import lax
from jax.experimental import pallas as pl
from jax.experimental.pallas import tpu as pltpu
from jax.sharding import PartitionSpec as P

NB = 16
AXES = ("row", "col")
VMEM_LIMIT = 48 * 1024 * 1024
HIGHEST = lax.Precision.HIGHEST


def tile_slots(rows, cols):
    return [
        (a, b)
        for a in reversed(range(NB // rows))
        for b in reversed(range(NB // cols))
        if a * rows + rows - 1 > b * cols
    ]


def send(array, rows, cols, target):
    pairs = []
    for r in range(rows):
        for c in range(cols):
            to_r, to_c = target(r, c)
            pairs.append((r * cols + c, to_r * cols + to_c))
    return lax.ppermute(array, AXES, pairs)


def along_z(array, rows, cols, step):
    return send(array, rows, cols, lambda r, c: ((r + 2 * step) % rows, c))


def along_col(array, rows, cols, step):
    return send(array, rows, cols, lambda r, c: (r, (c + step) % cols))


def other_core(array, rows, cols):
    return send(array, rows, cols, lambda r, c: (r ^ 1, c))


def fold_kernel(slots, panel_ref, inverse_ref, out_ref):
    for at, (a, b) in enumerate(slots):
        inverse = inverse_ref[b]
        high = inverse.astype(jnp.bfloat16)
        low = (inverse - high.astype(jnp.float32)).astype(jnp.bfloat16)
        tile = panel_ref[a, b]
        out_ref[at] = (
            jnp.dot(tile, high, preferred_element_type=jnp.float32)
            + jnp.dot(tile, low, preferred_element_type=jnp.float32)
        ).astype(jnp.bfloat16)


def fold_panel(panel, inverse, slots):
    bs = panel.shape[-1]
    return pl.pallas_call(
        functools.partial(fold_kernel, slots),
        out_shape=jax.ShapeDtypeStruct((len(slots), bs, bs), jnp.bfloat16),
        compiler_params=pltpu.CompilerParams(vmem_limit_bytes=VMEM_LIMIT),
        name="fold_panel",
    )(panel, inverse)


def segment_kernel(chunk, index_ref, tiles_ref, out_ref, sums):
    step = pl.program_id(0)
    blocks, bs = tiles_ref.shape[1], tiles_ref.shape[2]

    @pl.when(step == 0)
    def _():
        sums[...] = jnp.zeros_like(sums)

    for p in range(chunk):
        segment = index_ref[step * chunk + p]
        for b in range(blocks):
            cols = slice(b * bs, (b + 1) * bs)
            sums[segment, :, cols] += tiles_ref[p, b].astype(jnp.float32)

    @pl.when(step == pl.num_programs(0) - 1)
    def _():
        out_ref[...] = sums[...].astype(jnp.bfloat16)


def segment_sums(offdiag, row_index, segments):
    tiles, blocks, bs, _ = offdiag.shape
    chunk = 8
    return pl.pallas_call(
        functools.partial(segment_kernel, chunk),
        grid_spec=pltpu.PrefetchScalarGridSpec(
            num_scalar_prefetch=1,
            grid=(tiles // chunk,),
            in_specs=[pl.BlockSpec((chunk, blocks, bs, bs), lambda i, index: (i, 0, 0, 0))],
            out_specs=pl.BlockSpec((segments, bs, blocks * bs), lambda i, index: (0, 0, 0)),
            scratch_shapes=[pltpu.VMEM((segments, bs, blocks * bs), jnp.float32)],
        ),
        out_shape=jax.ShapeDtypeStruct((segments, bs, blocks * bs), jnp.bfloat16),
        compiler_params=pltpu.CompilerParams(vmem_limit_bytes=VMEM_LIMIT),
        cost_estimate=pl.CostEstimate(
            flops=offdiag.size, bytes_accessed=2 * offdiag.size, transcendentals=0
        ),
        name="segment_sums",
    )(row_index, offdiag)


def update_kernel(cols, *refs):
    known_refs, (sums_ref, rhs_ref, inverse_ref, keep_ref, give_ref, whole) = refs[:cols], refs[cols:]
    blocks, count, bs = rhs_ref.shape
    per = known_refs[0].shape[0]
    row_id, col_id = lax.axis_index("row"), lax.axis_index("col")
    off = jnp.zeros((count, blocks * bs), jnp.float32)
    for step in range(cols):
        first = lax.rem(col_id + cols - step, cols) * per
        for i in range(per):
            off += jnp.dot(
                known_refs[step][i], sums_ref[first + i], preferred_element_type=jnp.float32
            )
    adds = (row_id == 0).astype(jnp.float32)
    for b in range(blocks):
        total = rhs_ref[b] * adds - off[:, b * bs : (b + 1) * bs]
        whole[b] = jnp.dot(
            total, inverse_ref[b], precision=HIGHEST, preferred_element_type=jnp.float32
        )
    half = count // 2
    core = lax.rem(row_id, 2)
    keep = pl.ds(pl.multiple_of(core * half, half), half)
    give = pl.ds(pl.multiple_of((1 - core) * half, half), half)
    keep_ref[...] = whole[:, keep, :]
    give_ref[...] = whole[:, give, :].astype(jnp.bfloat16)


def local_update(known, sums, rhs, inverse):
    blocks, count, bs = rhs.shape
    half = (blocks, count // 2, bs)
    return pl.pallas_call(
        functools.partial(update_kernel, len(known)),
        out_shape=(
            jax.ShapeDtypeStruct(half, jnp.float32),
            jax.ShapeDtypeStruct(half, jnp.bfloat16),
        ),
        scratch_shapes=[pltpu.VMEM(rhs.shape, jnp.float32)],
        compiler_params=pltpu.CompilerParams(vmem_limit_bytes=VMEM_LIMIT),
        name="local_update",
    )(*known, sums, rhs, inverse)


def span(slots, rows, cols, wanted):
    found = [
        at
        for at, (a, b) in enumerate(slots)
        for r in range(rows)
        for c in range(cols)
        if a * rows + r > b * cols + c and wanted(a * rows + r, b * cols + c)
    ]
    return min(found), max(found) + 1 - min(found)


def make_plan(rows, cols):
    half = NB // 2
    slots = tile_slots(rows, cols)
    return dict(
        rows=rows,
        cols=cols,
        slots=slots,
        high=span(slots, rows, cols, lambda j, k: k >= half),
        cross=span(slots, rows, cols, lambda j, k: j >= half > k),
        low=span(slots, rows, cols, lambda j, k: j < half),
        upper=(half // cols, NB // cols - half // cols),
        lower=(0, -(-half // cols)),
    )


def solve_half(sums, tile, first, solved):
    for i in reversed(range(len(sums))):
        block = sums[i].astype(jnp.bfloat16)
        solved[i] = block
        for m in reversed(range(i)):
            sums[m] = sums[m] - jnp.dot(
                block, tile(first + i, first + m), preferred_element_type=jnp.float32
            )


def place(refs, into, cols, col_id):
    for step, ref in enumerate(refs):
        owner = lax.rem(col_id + cols - step, cols)
        for b in range(ref.shape[0]):
            into[b * cols + owner] = ref[b].astype(jnp.float32)


def start_tiles(plan, part, line_ref, mine, theirs, tiles, sems):
    cols = plan["cols"]
    col_id, core = lax.axis_index("col"), lax.rem(lax.axis_index("row"), 2)
    first, count = plan[part]
    pairs = [(line_ref.at[:, :, pl.ds(first, count)], tiles.at[:, :, col_id])]
    for step in range(1, cols):
        owner = lax.rem(col_id + cols - step, cols)
        pairs.append((mine[step - 1], tiles.at[:, core, owner]))
        pairs.append((theirs[step - 1], tiles.at[:, 1 - core, owner]))
    copies = [pltpu.make_async_copy(a, b, sems.at[i]) for i, (a, b) in enumerate(pairs)]
    for copy in copies:
        copy.start()
    return copies


def tile_reader(plan, part, tiles):
    def read(j, k):
        at = plan["slots"].index((j // plan["rows"], k // plan["cols"])) - plan[part][0]
        r = j % plan["rows"]
        return tiles[r // 2, r % 2, k % plan["cols"], at]

    return read


def upper_kernel(plan, *refs):
    rows, cols = plan["rows"], plan["cols"]
    half, others = NB // 2, cols - 1
    value_refs, refs = refs[:cols], refs[cols:]
    own_ref, line_ref, refs = refs[0], refs[1], refs[2:]
    mine, theirs, refs = refs[:others], refs[others : 2 * others], refs[2 * others :]
    solved, lower_ref, tiles, cross, values, sems = refs
    copies = start_tiles(plan, "high", line_ref, mine, theirs, tiles, sems)
    wanted = line_ref.at[:, :, pl.ds(*plan["cross"])]
    copies.append(pltpu.make_async_copy(wanted, cross, sems.at[len(copies)]))
    copies[-1].start()
    place(value_refs, values, cols, lax.axis_index("col"))
    for copy in copies:
        copy.wait()
    skip = plan["upper"][0] * cols
    sums = [values[half + i - skip] for i in range(half)]
    solve_half(sums, tile_reader(plan, "high", tiles), half, solved)
    for b in range(plan["lower"][1]):
        total = own_ref[b]
        for j in range(half, NB):
            at = plan["slots"].index((j // rows, b)) - plan["cross"][0]
            r = j % rows
            total = total - jnp.dot(
                solved[j - half], cross[r // 2, r % 2, at], preferred_element_type=jnp.float32
            )
        lower_ref[b] = total.astype(jnp.bfloat16)


def lower_kernel(plan, *refs):
    cols = plan["cols"]
    half, others = NB // 2, cols - 1
    value_refs, refs = refs[:cols], refs[cols:]
    upper_ref, line_ref, refs = refs[0], refs[1], refs[2:]
    mine, theirs, refs = refs[:others], refs[others : 2 * others], refs[2 * others :]
    out_ref, tiles, values, solved, sems = refs
    copies = start_tiles(plan, "low", line_ref, mine, theirs, tiles, sems)
    col_id = lax.axis_index("col")
    place(value_refs, values, cols, col_id)
    solved[pl.ds(half, half)] = upper_ref[...]
    for copy in copies:
        copy.wait()
    sums = [values[i] for i in range(half)]
    solve_half(sums, tile_reader(plan, "low", tiles), 0, solved)
    for b in range(out_ref.shape[0]):
        out_ref[b] = solved[b * cols + col_id]


def call_half(kernel, plan, part, values, extra, line, mine, theirs, out_shape, scratch):
    rows, cols = plan["rows"], plan["cols"]
    bs = line.shape[-1]
    blocks, count, _ = values[0].shape
    vmem, anywhere = (pl.BlockSpec(memory_space=m) for m in (pltpu.VMEM, pl.ANY))
    return pl.pallas_call(
        functools.partial(kernel, plan),
        in_specs=[vmem] * (cols + 1) + [anywhere] * (1 + len(mine) + len(theirs)),
        out_specs=jax.tree.map(lambda _: vmem, out_shape),
        out_shape=out_shape,
        scratch_shapes=[
            pltpu.VMEM((rows // 2, 2, cols, plan[part][1], bs, bs), jnp.bfloat16),
            *scratch,
            pltpu.SemaphoreType.DMA((2 * cols,)),
        ],
        compiler_params=pltpu.CompilerParams(vmem_limit_bytes=VMEM_LIMIT),
        name=part + "_half",
    )(*values, extra, line, *mine, *theirs)


def upper_half(plan, values, own, line, mine, theirs):
    rows, cols, half = plan["rows"], plan["cols"], NB // 2
    bs, count = line.shape[-1], own.shape[1]
    return call_half(
        upper_kernel, plan, "high", values, own, line, mine, theirs,
        (
            jax.ShapeDtypeStruct((half, count, bs), jnp.bfloat16),
            jax.ShapeDtypeStruct(own.shape, jnp.bfloat16),
        ),
        [
            pltpu.VMEM((rows // 2, 2, plan["cross"][1], bs, bs), jnp.bfloat16),
            pltpu.VMEM((plan["upper"][1] * cols, count, bs), jnp.float32),
        ],
    )


def lower_half(plan, values, upper, line, mine, theirs):
    cols, bs, count = plan["cols"], line.shape[-1], upper.shape[1]
    return call_half(
        lower_kernel, plan, "low", values, upper, line, mine, theirs,
        jax.ShapeDtypeStruct((NB // cols, count, bs), jnp.bfloat16),
        [
            pltpu.VMEM((plan["lower"][1] * cols, count, bs), jnp.float32),
            pltpu.VMEM((NB, count, bs), jnp.bfloat16),
        ],
    )


def gather_tiles(plan, part, line, core):
    rows, cols = plan["rows"], plan["cols"]
    first, count = plan[part]
    piece = lax.dynamic_index_in_dim(line, core, 1, keepdims=False)[:, first : first + count]
    mine = [along_col(piece, rows, cols, d) for d in range(1, cols)]
    return mine, [other_core(got, rows, cols) for got in mine]


def body(rhs, diag_inv, panel, offdiag, known, row_index):
    rows, cols = lax.axis_size("row"), lax.axis_size("col")
    plan = make_plan(rows, cols)
    core = lax.rem(lax.axis_index("row"), 2)

    folded = fold_panel(panel, diag_inv, plan["slots"])
    line = lax.all_gather(folded, "row", axis=0)
    line = line.reshape(rows // 2, 2, *folded.shape)
    known_all = [known] + [along_col(known, rows, cols, d) for d in range(1, cols)]

    sums = segment_sums(offdiag, row_index, known.shape[0] * cols)
    keep, give = local_update(known_all, sums, rhs, diag_inv)
    part = (keep + other_core(give, rows, cols).astype(jnp.float32)).astype(jnp.bfloat16)
    parts = [part] + [along_z(part, rows, cols, d) for d in range(1, rows // 2)]
    total = sum(p.astype(jnp.float32) for p in parts)
    first, count = plan["upper"]
    upper = total[first : first + count].astype(jnp.bfloat16)
    values = [upper] + [along_col(upper, rows, cols, d) for d in range(1, cols)]

    high = gather_tiles(plan, "high", line, core)
    low = gather_tiles(plan, "low", line, core)
    solved, lower = upper_half(plan, values, total[: plan["lower"][1]], line, *high)
    values = [lower] + [along_col(lower, rows, cols, d) for d in range(1, cols)]
    mine = lower_half(plan, values, solved, line, *low)
    theirs = other_core(mine, rows, cols)
    return jnp.concatenate(
        [jnp.where(core == 0, mine, theirs), jnp.where(core == 0, theirs, mine)], axis=1
    )


def solution(mesh):
    placed = (
        P("col", None, None),
        P("col", None, None),
        P("row", "col", None, None),
        P("row", "col", None, None),
        P(("row", "col"), None, None),
        P("row"),
    )
    return jax.shard_map(
        body, mesh=mesh, in_specs=placed, out_specs=P("col", None, None), check_vma=False
    )
```

```python
import functools

import jax
import jax.numpy as jnp
from jax import lax
from jax.experimental import pallas as pl
from jax.experimental.pallas import tpu as pltpu
from jax.sharding import PartitionSpec as P

NB = 16
AXES = ("row", "col")
VMEM_LIMIT = 16 * 1024 * 1024
HIGHEST = lax.Precision.HIGHEST


class Plan:
    def __init__(self, rows, cols):
        self.rows, self.cols, self.zs = rows, cols, rows // 2
        self.slots = [
            (a, b)
            for a in reversed(range(NB // rows))
            for b in reversed(range(NB // cols))
            if a * rows + rows - 1 > b * cols
        ]
        self.lists = {
            (core, c): [
                (r, at)
                for r in range(core, rows, 2)
                for at, (a, b) in enumerate(self.slots)
                if a * rows + r > b * cols + c
            ]
            for core in range(2)
            for c in range(cols)
        }
        self.packed = max(2, *map(len, self.lists.values()))
        self.cut = self.packed // 2
        self.flips = [1 << i for i in range(cols.bit_length() - 1)]
        self.solvers = sorted({max(self.zs // 2 - 1, 0), self.zs // 2})


def send(array, plan, pairs):
    flat = [(r * plan.cols + c, to_r * plan.cols + to_c) for (r, c), (to_r, to_c) in pairs]
    return lax.ppermute(array, AXES, flat)


def across_z(array, plan, flip):
    to = {z ^ flip: z for z in plan.solvers}
    free = [z for z in range(plan.zs) if z not in to.values()]
    for z in range(plan.zs):
        if z not in to:
            to[z] = min(free, key=lambda other: abs(other - z))
            free.remove(to[z])
    pairs = [
        ((2 * z + core, c), (2 * to[z] + core, c))
        for z in range(plan.zs)
        for core in range(2)
        for c in range(plan.cols)
    ]
    return send(array, plan, pairs)


def out_of_solvers(array, plan):
    low, high = plan.solvers[0], plan.solvers[-1]
    z = lax.axis_index("row") // 2
    for step in range(1, plan.zs // 2):
        to = {low: low - step, high: high + step, low - step: low, high + step: high}
        pairs = [
            ((2 * a + core, c), (2 * to.get(a, a) + core, c))
            for a in range(plan.zs)
            for core in range(2)
            for c in range(plan.cols)
        ]
        got = send(array, plan, pairs)
        array = jnp.where(jnp.logical_or(z == low - step, z == high + step), got, array)
    return array


def across_col(array, plan, flip):
    pairs = [((r, c), (r, c ^ flip)) for r in range(plan.rows) for c in range(plan.cols)]
    return send(array, plan, pairs)


def other_core(array, plan):
    pairs = [((r, c), (r ^ 1, c)) for r in range(plan.rows) for c in range(plan.cols)]
    return send(array, plan, pairs)


def direct(array, plan):
    return jnp.stack([array] + [across_col(array, plan, m) for m in range(1, plan.cols)])


NO_COST = pl.CostEstimate(flops=0, bytes_accessed=0, transcendentals=0)


def fold_kernel(slots, panel_hbm, inverse_hbm, out_ref, panel_ref, inverse_ref, sems):
    copies = [
        pltpu.make_async_copy(inverse_hbm, inverse_ref, sems.at[0]),
        pltpu.make_async_copy(panel_hbm, panel_ref, sems.at[1]),
    ]
    for copy in copies:
        copy.start()
    for copy in copies:
        copy.wait()
    for at, (a, b) in enumerate(slots):
        inverse = inverse_ref[b]
        high = inverse.astype(jnp.bfloat16)
        low = (inverse - high.astype(jnp.float32)).astype(jnp.bfloat16)
        tile = panel_ref[a, b]
        out_ref[at] = (
            jnp.dot(tile, high, preferred_element_type=jnp.float32)
            + jnp.dot(tile, low, preferred_element_type=jnp.float32)
        ).astype(jnp.bfloat16)


def fold_panel(panel, inverse, slots):
    bs = panel.shape[-1]
    return pl.pallas_call(
        functools.partial(fold_kernel, slots),
        in_specs=[pl.BlockSpec(memory_space=pltpu.HBM)] * 2,
        out_shape=jax.ShapeDtypeStruct((len(slots), bs, bs), jnp.bfloat16),
        scratch_shapes=[
            pltpu.VMEM(panel.shape, panel.dtype),
            pltpu.VMEM(inverse.shape, inverse.dtype),
            pltpu.SemaphoreType.DMA((2,)),
        ],
        compiler_params=pltpu.CompilerParams(vmem_limit_bytes=62 * 1024 * 1024),
        cost_estimate=NO_COST,
        name="fold_panel",
    )(panel, inverse)


def segment_kernel(chunk, index_ref, tiles_hbm, out_ref, tiles, sums, sems):
    copies = [
        pltpu.make_async_copy(
            tiles_hbm.at[pl.ds(i * chunk, chunk)], tiles.at[pl.ds(i * chunk, chunk)], sems.at[i]
        )
        for i in range(tiles.shape[0] // chunk)
    ]
    for copy in copies:
        copy.start()
    sums[...] = jnp.zeros_like(sums)
    for i, copy in enumerate(copies):
        copy.wait()

        def add(p, carry):
            sums[index_ref[p]] += tiles[p].astype(jnp.float32)
            return carry

        lax.fori_loop(i * chunk, (i + 1) * chunk, add, 0)
    out_ref[...] = sums[...].astype(jnp.bfloat16)


def segment_sums(offdiag, row_index, segments):
    tiles, blocks, bs, _ = offdiag.shape
    chunk = 4
    return pl.pallas_call(
        functools.partial(segment_kernel, chunk),
        in_specs=[pl.BlockSpec(memory_space=pltpu.SMEM), pl.BlockSpec(memory_space=pltpu.HBM)],
        out_shape=jax.ShapeDtypeStruct((segments, blocks, bs, bs), jnp.bfloat16),
        scratch_shapes=[
            pltpu.VMEM(offdiag.shape, offdiag.dtype),
            pltpu.VMEM((segments, blocks, bs, bs), jnp.float32),
            pltpu.SemaphoreType.DMA((tiles // chunk,)),
        ],
        compiler_params=pltpu.CompilerParams(vmem_limit_bytes=58 * 1024 * 1024),
        cost_estimate=pl.CostEstimate(
            flops=offdiag.size, bytes_accessed=2 * offdiag.size, transcendentals=0
        ),
        name="segment_sums",
    )(row_index, offdiag)


def update_kernel(known_ref, sums_ref, rhs_ref, inverse_ref, keep_ref, give_ref, whole):
    blocks, count, bs = rhs_ref.shape
    cols, per = known_ref.shape[:2]
    row_id, col_id = lax.axis_index("row"), lax.axis_index("col")
    off = [jnp.zeros((count, bs), jnp.float32)] * blocks
    for step in range(cols):
        first = lax.bitwise_xor(col_id, step) * per
        for i in range(per):
            for b in range(blocks):
                off[b] += jnp.dot(
                    known_ref[step, i], sums_ref[first + i, b], preferred_element_type=jnp.float32
                )
    adds = (row_id == 0).astype(jnp.float32)
    for b in range(blocks):
        total = rhs_ref[b] * adds - off[b]
        whole[b] = jnp.dot(
            total, inverse_ref[b], precision=HIGHEST, preferred_element_type=jnp.float32
        )
    half = count // 2
    core = lax.rem(row_id, 2)
    keep = pl.ds(pl.multiple_of(core * half, half), half)
    give = pl.ds(pl.multiple_of((1 - core) * half, half), half)
    keep_ref[...] = whole[:, keep, :]
    give_ref[...] = whole[:, give, :].astype(jnp.bfloat16)


def local_update(known, sums, rhs, inverse):
    blocks, count, bs = rhs.shape
    half = (blocks, count // 2, bs)
    return pl.pallas_call(
        update_kernel,
        out_shape=(
            jax.ShapeDtypeStruct(half, jnp.float32),
            jax.ShapeDtypeStruct(half, jnp.bfloat16),
        ),
        scratch_shapes=[pltpu.VMEM(rhs.shape, jnp.float32)],
        compiler_params=pltpu.CompilerParams(vmem_limit_bytes=VMEM_LIMIT),
        cost_estimate=NO_COST,
        name="local_update",
    )(known, sums, rhs, inverse)


def pack_kernel(plan, *refs):
    line_refs, (first_ref, second_ref) = refs[: plan.zs], refs[plan.zs :]
    row_id, col_id = lax.axis_index("row"), lax.axis_index("col")
    core, z = lax.rem(row_id, 2), row_id // 2
    for i in range(plan.packed):
        into = first_ref.at[i] if i < plan.cut else second_ref.at[i - plan.cut]
        back, at = jnp.int32(0), jnp.int32(0)
        for (side, c), found in plan.lists.items():
            if i < len(found):
                mine = jnp.logical_and(col_id == c, core == side)
                back = jnp.where(mine, lax.bitwise_xor(z, found[i][0] // 2), back)
                at = jnp.where(mine, found[i][1], at)
        for step, line_ref in enumerate(line_refs):

            @pl.when(back == step)
            def _():
                into[...] = line_ref[at]


def pack(plan, line):
    bs = line[0].shape[-1]
    return pl.pallas_call(
        functools.partial(pack_kernel, plan),
        out_shape=[
            jax.ShapeDtypeStruct((count, bs, bs), jnp.bfloat16)
            for count in (plan.cut, plan.packed - plan.cut)
        ],
        compiler_params=pltpu.CompilerParams(vmem_limit_bytes=VMEM_LIMIT),
        cost_estimate=NO_COST,
        name="pack",
    )(*line)


def chain_kernel(plan, value_ref, *refs):
    rows, cols = plan.rows, plan.cols
    first_ref, second_ref, out_ref, values, solved = refs
    row_id, col_id = lax.axis_index("row"), lax.axis_index("col")
    core = lax.rem(row_id, 2)
    for step in range(cols):
        owner = lax.bitwise_xor(col_id, step)
        for b in range(value_ref.shape[1]):
            values[b * cols + owner] = value_ref[step, b].astype(jnp.float32)

    steps, turned = [], []
    for c in range(cols):
        step = lax.bitwise_xor(col_id, c)
        steps.append(step)
        turned.append(
            sum(
                lax.rem(step // flip, 2) * other
                for flip, other in zip(plan.flips, reversed(plan.flips))
            )
        )

    def tile(j, k):
        r, c = j % rows, k % cols
        at = plan.lists[r % 2, c].index((r, plan.slots.index((j // rows, k // cols))))
        side = lax.bitwise_xor(core, r % 2)
        if at < plan.cut:
            return first_ref[side, steps[c], at]
        return second_ref[side, turned[c], at - plan.cut]

    sums = [values[k] for k in range(NB)]
    for j in reversed(range(NB)):
        block = sums[j].astype(jnp.bfloat16)
        solved[j] = block
        for k in reversed(range(j)):
            sums[k] = sums[k] - jnp.dot(block, tile(j, k), preferred_element_type=jnp.float32)
    for b in range(out_ref.shape[0]):
        out_ref[b] = solved[b * cols + col_id]


def chain(plan, values, first, second):
    _, per, count, bs = values.shape
    return pl.pallas_call(
        functools.partial(chain_kernel, plan),
        out_shape=jax.ShapeDtypeStruct((per, count, bs), jnp.bfloat16),
        scratch_shapes=[
            pltpu.VMEM((NB, count, bs), jnp.float32),
            pltpu.VMEM((NB, count, bs), jnp.bfloat16),
        ],
        compiler_params=pltpu.CompilerParams(vmem_limit_bytes=VMEM_LIMIT),
        cost_estimate=NO_COST,
        name="chain",
    )(values, first, second)


def after(array, *done):
    return lax.optimization_barrier((array, *done))[0]


def body(rhs, diag_inv, panel, offdiag, known, row_index):
    plan = Plan(lax.axis_size("row"), lax.axis_size("col"))
    core = lax.rem(lax.axis_index("row"), 2)

    known_all = direct(known, plan)
    folded = fold_panel(panel, diag_inv, plan.slots)
    line = [folded] + [across_z(folded, plan, m) for m in range(1, plan.zs)]
    sums = segment_sums(offdiag, row_index, known.shape[0] * plan.cols)
    keep, give = local_update(known_all, sums, rhs, diag_inv)
    first, second = pack(plan, [after(piece, sums) for piece in line])

    part = (keep + other_core(give, plan).astype(jnp.float32)).astype(jnp.bfloat16)
    parts = [part] + [across_z(part, plan, m) for m in range(1, plan.zs)]
    total = sum(p.astype(jnp.float32) for p in parts).astype(jnp.bfloat16)
    values = direct(total, plan)

    halves = []
    for half, flips in ((first, plan.flips), (second, plan.flips[::-1])):
        mine, theirs = [half[None]], []
        for step, flip in enumerate(flips):
            held = mine[0] if len(mine) == 1 else jnp.concatenate(mine)
            if step == len(flips) - 1:
                held = after(held, total)
                theirs.append(other_core(held, plan))
            mine = [held, across_col(held, plan, flip)]
        theirs.append(other_core(after(mine[1], values), plan))
        halves.append(jnp.stack([jnp.concatenate(mine), jnp.concatenate(theirs)]))

    mine = out_of_solvers(chain(plan, values, *halves), plan)
    theirs = other_core(mine, plan)
    return jnp.concatenate(
        [jnp.where(core == 0, mine, theirs), jnp.where(core == 0, theirs, mine)], axis=1
    )


def solution(mesh):
    placed = (
        P("col", None, None),
        P("col", None, None),
        P("row", "col", None, None),
        P("row", "col", None, None),
        P(("row", "col"), None, None),
        P("row"),
    )
    return jax.shard_map(
        body, mesh=mesh, in_specs=placed, out_specs=P("col", None, None), check_vma=False
    )
```

```python
import functools

import jax
import jax.numpy as jnp
from jax import lax
from jax.experimental import pallas as pl
from jax.experimental.pallas import tpu as pltpu
from jax.sharding import PartitionSpec as P

NB = 16
AXES = ("row", "col")
VMEM_LIMIT = 16 * 1024 * 1024
HIGHEST = lax.Precision.HIGHEST


class Plan:
    def __init__(self, rows, cols):
        self.rows, self.cols, self.zs = rows, cols, rows // 2
        self.slots = [
            (a, b)
            for a in reversed(range(NB // rows))
            for b in reversed(range(NB // cols))
            if a * rows + rows - 1 > b * cols
        ]
        half = NB // 2
        self.high, self.low, self.cross = {}, {}, {}
        for core in range(2):
            for c in range(cols):
                below = [
                    (r, at, a * rows + r, b * cols + c)
                    for r in range(core, rows, 2)
                    for at, (a, b) in enumerate(self.slots)
                    if a * rows + r > b * cols + c
                ]
                self.high[core, c] = [t[:2] for t in below if t[3] >= half]
                self.low[core, c] = [t[:2] for t in below if t[2] < half]
                self.cross[core, c] = [t[:2] for t in below if t[2] >= half > t[3]]
        self.lists = (self.high, self.low, self.cross)
        self.counts = [max(map(len, lists.values())) for lists in self.lists]
        self.upper = slice(half // cols, NB // cols)
        self.lower = slice(0, -(-half // cols))
        self.solvers = sorted({max(self.zs // 2 - 1, 0), self.zs // 2})
        self.arrival = [self.zs - 1, *range(1, self.zs - 1), 0]


def send(array, plan, pairs):
    flat = [(r * plan.cols + c, to_r * plan.cols + to_c) for (r, c), (to_r, to_c) in pairs]
    return lax.ppermute(array, AXES, flat)


def across_z(array, plan, flip):
    to = {z ^ flip: z for z in plan.solvers}
    free = [z for z in range(plan.zs) if z not in to.values()]
    for z in range(plan.zs):
        if z not in to:
            to[z] = min(free, key=lambda other: abs(other - z))
            free.remove(to[z])
    pairs = [
        ((2 * z + core, c), (2 * to[z] + core, c))
        for z in range(plan.zs)
        for core in range(2)
        for c in range(plan.cols)
    ]
    return send(array, plan, pairs)


def out_of_solvers(array, plan):
    low, high = plan.solvers[0], plan.solvers[-1]
    z = lax.axis_index("row") // 2
    own, other = array, other_core(array, plan)
    for step in range(1, plan.zs // 2):
        to = {low: low - step, high: high + step, low - step: low, high + step: high}
        outer = jnp.logical_or(z == low - step, z == high + step)
        got = []
        for cross in range(2):
            pairs = [
                ((2 * a + core, c), (2 * to.get(a, a) + (core ^ cross), c))
                for a in range(plan.zs)
                for core in range(2)
                for c in range(plan.cols)
            ]
            got.append(send(array, plan, pairs))
        own, other = jnp.where(outer, got[0], own), jnp.where(outer, got[1], other)
    return own, other


def across_col(array, plan, flip):
    pairs = [((r, c), (r, c ^ flip)) for r in range(plan.rows) for c in range(plan.cols)]
    return send(array, plan, pairs)


def other_core(array, plan):
    pairs = [((r, c), (r ^ 1, c)) for r in range(plan.rows) for c in range(plan.cols)]
    return send(array, plan, pairs)


def spread(array, plan):
    return lax.all_to_all(jnp.broadcast_to(array, (plan.cols, *array.shape)), "col", 0, 0)


def direct(array, plan):
    return [array] + [across_col(array, plan, m) for m in range(1, plan.cols)]


NO_COST = pl.CostEstimate(flops=0, bytes_accessed=0, transcendentals=0)


def fold_kernel(slots, panel_hbm, inverse_hbm, known_hbm, out_ref, known_ref, panel_ref, inverse_ref, sems):
    copies = [
        pltpu.make_async_copy(inverse_hbm, inverse_ref, sems.at[0]),
        pltpu.make_async_copy(panel_hbm, panel_ref, sems.at[1]),
    ]
    copies += [
        pltpu.make_async_copy(known_hbm, known_ref.at[c], sems.at[2 + c])
        for c in range(known_ref.shape[0])
    ]
    for copy in copies:
        copy.start()
    for copy in copies:
        copy.wait()
    for at, (a, b) in enumerate(slots):
        inverse = inverse_ref[b]
        high = inverse.astype(jnp.bfloat16)
        low = (inverse - high.astype(jnp.float32)).astype(jnp.bfloat16)
        tile = panel_ref[a, b]
        out_ref[at] = (
            jnp.dot(tile, high, preferred_element_type=jnp.float32)
            + jnp.dot(tile, low, preferred_element_type=jnp.float32)
        ).astype(jnp.bfloat16)


def fold_panel(panel, inverse, known, slots, cols):
    bs = panel.shape[-1]
    return pl.pallas_call(
        functools.partial(fold_kernel, slots),
        in_specs=[pl.BlockSpec(memory_space=pltpu.HBM)] * 3,
        out_shape=(
            jax.ShapeDtypeStruct((len(slots), bs, bs), jnp.bfloat16),
            jax.ShapeDtypeStruct((cols, *known.shape), known.dtype),
        ),
        scratch_shapes=[
            pltpu.VMEM(panel.shape, panel.dtype),
            pltpu.VMEM(inverse.shape, inverse.dtype),
            pltpu.SemaphoreType.DMA((2 + cols,)),
        ],
        compiler_params=pltpu.CompilerParams(vmem_limit_bytes=62 * 1024 * 1024),
        cost_estimate=NO_COST,
        name="fold_panel",
    )(panel, inverse, known)


def segment_kernel(chunk, index_ref, tiles_hbm, out_ref, tiles, sums, sems):
    copies = [
        pltpu.make_async_copy(
            tiles_hbm.at[pl.ds(i * chunk, chunk)], tiles.at[pl.ds(i * chunk, chunk)], sems.at[i]
        )
        for i in range(tiles.shape[0] // chunk)
    ]
    for copy in copies:
        copy.start()
    sums[...] = jnp.zeros_like(sums)
    for i, copy in enumerate(copies):
        copy.wait()

        def add(p, carry):
            sums[index_ref[p]] += tiles[p].astype(jnp.float32)
            return carry

        lax.fori_loop(i * chunk, (i + 1) * chunk, add, 0)
    out_ref[...] = sums[...].astype(jnp.bfloat16)


def segment_sums(offdiag, row_index, segments):
    tiles, blocks, bs, _ = offdiag.shape
    chunk = 4
    return pl.pallas_call(
        functools.partial(segment_kernel, chunk),
        in_specs=[pl.BlockSpec(memory_space=pltpu.SMEM), pl.BlockSpec(memory_space=pltpu.HBM)],
        out_shape=jax.ShapeDtypeStruct((segments, blocks, bs, bs), jnp.bfloat16),
        scratch_shapes=[
            pltpu.VMEM(offdiag.shape, offdiag.dtype),
            pltpu.VMEM((segments, blocks, bs, bs), jnp.float32),
            pltpu.SemaphoreType.DMA((tiles // chunk,)),
        ],
        compiler_params=pltpu.CompilerParams(vmem_limit_bytes=52 * 1024 * 1024),
        cost_estimate=pl.CostEstimate(
            flops=offdiag.size, bytes_accessed=2 * offdiag.size, transcendentals=0
        ),
        name="segment_sums",
    )(row_index, offdiag)


def update_kernel(known_ref, sums_ref, rhs_ref, inverse_ref, keep_ref, give_ref, whole):
    blocks, count, bs = rhs_ref.shape
    cols, per = known_ref.shape[:2]
    row_id = lax.axis_index("row")
    off = [jnp.zeros((count, bs), jnp.float32)] * blocks
    for c in range(cols):
        for i in range(per):
            for b in range(blocks):
                off[b] += jnp.dot(
                    known_ref[c, i], sums_ref[c * per + i, b], preferred_element_type=jnp.float32
                )
    adds = (row_id == 0).astype(jnp.float32)
    for b in range(blocks):
        total = rhs_ref[b] * adds - off[b]
        whole[b] = jnp.dot(
            total, inverse_ref[b], precision=HIGHEST, preferred_element_type=jnp.float32
        )
    half = count // 2
    core = lax.rem(row_id, 2)
    keep = pl.ds(pl.multiple_of(core * half, half), half)
    give = pl.ds(pl.multiple_of((1 - core) * half, half), half)
    keep_ref[...] = whole[:, keep, :]
    give_ref[...] = whole[:, give, :].astype(jnp.bfloat16)


def local_update(known, sums, rhs, inverse):
    blocks, count, bs = rhs.shape
    half = (blocks, count // 2, bs)
    return pl.pallas_call(
        update_kernel,
        out_shape=(
            jax.ShapeDtypeStruct(half, jnp.float32),
            jax.ShapeDtypeStruct(half, jnp.bfloat16),
        ),
        scratch_shapes=[pltpu.VMEM(rhs.shape, jnp.float32)],
        compiler_params=pltpu.CompilerParams(vmem_limit_bytes=VMEM_LIMIT),
        cost_estimate=NO_COST,
        name="local_update",
    )(known, sums, rhs, inverse)


def pack_kernel(plan, *refs):
    line_refs = [refs[plan.arrival.index(step)] for step in range(plan.zs)]
    row_id, col_id = lax.axis_index("row"), lax.axis_index("col")
    core, z = lax.rem(row_id, 2), row_id // 2
    within_ref, cross_ref = refs[plan.zs :]
    for which, (lists, count) in enumerate(zip(plan.lists, plan.counts)):
        out_ref = cross_ref if which == 2 else within_ref
        first = plan.counts[0] if which == 1 else 0
        for i in range(count):
            back, at = jnp.int32(0), jnp.int32(0)
            for (side, c), found in lists.items():
                if i < len(found):
                    mine = jnp.logical_and(col_id == c, core == side)
                    back = jnp.where(mine, lax.bitwise_xor(z, found[i][0] // 2), back)
                    at = jnp.where(mine, found[i][1], at)
            for step, line_ref in enumerate(line_refs):

                @pl.when(back == step)
                def _():
                    out_ref[first + i] = line_ref[at]


def pack(plan, line):
    bs = line[0].shape[-1]
    return pl.pallas_call(
        functools.partial(pack_kernel, plan),
        out_shape=[
            jax.ShapeDtypeStruct((count, bs, bs), jnp.bfloat16)
            for count in (sum(plan.counts[:2]), plan.counts[2])
        ],
        compiler_params=pltpu.CompilerParams(vmem_limit_bytes=VMEM_LIMIT),
        cost_estimate=NO_COST,
        name="pack",
    )(*[line[step] for step in plan.arrival])


def solve(plan, value_ref, tiles_ref, values, solved, first):
    rows, cols, half = plan.rows, plan.cols, NB // 2
    core, col_id = lax.rem(lax.axis_index("row"), 2), lax.axis_index("col")
    for step in range(cols):
        owner = lax.bitwise_xor(col_id, step)
        for b in range(value_ref.shape[1]):
            values[b * cols + owner] = value_ref[step, b].astype(jnp.float32)

    def tile(j, k):
        r, c = j % rows, k % cols
        lists = plan.high if first else plan.low
        at = lists[r % 2, c].index((r, plan.slots.index((j // rows, k // cols))))
        return tiles_ref[lax.bitwise_xor(core, r % 2), c, at]

    skip = first // cols * cols
    sums = [values[first - skip + i] for i in range(half)]
    for i in reversed(range(half)):
        block = sums[i].astype(jnp.bfloat16)
        solved[first + i] = block
        for m in reversed(range(i)):
            sums[m] = sums[m] - jnp.dot(
                block, tile(first + i, first + m), preferred_element_type=jnp.float32
            )


def upper_kernel(plan, value_ref, own_ref, tiles_ref, cross_ref, out_ref, lower_ref, values, solved):
    rows, half = plan.rows, NB // 2
    core = lax.rem(lax.axis_index("row"), 2)
    solve(plan, value_ref, tiles_ref, values, solved, half)
    out_ref[...] = solved[pl.ds(half, half)]
    for b in range(own_ref.shape[0]):
        total = own_ref[b]
        for j in range(half, NB):
            r = j % rows
            at = plan.cross[r % 2, 0].index((r, plan.slots.index((j // rows, b))))
            tile = cross_ref[lax.bitwise_xor(core, r % 2), at]
            total = total - jnp.dot(solved[j], tile, preferred_element_type=jnp.float32)
        lower_ref[b] = total.astype(jnp.bfloat16)


def lower_kernel(plan, value_ref, upper_ref, tiles_ref, out_ref, values, solved):
    half, col_id = NB // 2, lax.axis_index("col")
    solved[pl.ds(half, half)] = upper_ref[...]
    solve(plan, value_ref, tiles_ref, values, solved, 0)
    for b in range(out_ref.shape[0]):
        out_ref[b] = solved[b * plan.cols + col_id]


def call_half(kernel, plan, name, out_shape, values, *args):
    _, blocks, count, bs = values.shape
    return pl.pallas_call(
        functools.partial(kernel, plan),
        out_shape=[jax.ShapeDtypeStruct((n, count, bs), jnp.bfloat16) for n in out_shape],
        scratch_shapes=[
            pltpu.VMEM((blocks * plan.cols, count, bs), jnp.float32),
            pltpu.VMEM((NB, count, bs), jnp.bfloat16),
        ],
        compiler_params=pltpu.CompilerParams(vmem_limit_bytes=VMEM_LIMIT),
        cost_estimate=NO_COST,
        name=name,
    )(values, *args)


def after(array, *done):
    return lax.optimization_barrier((array, *done))[0]


def body(rhs, diag_inv, panel, offdiag, known, row_index):
    plan = Plan(lax.axis_size("row"), lax.axis_size("col"))
    core = lax.rem(lax.axis_index("row"), 2)

    folded, known = fold_panel(panel, diag_inv, known, plan.slots, plan.cols)
    line = [folded] + [across_z(folded, plan, m) for m in range(1, plan.zs)]
    known_all = lax.all_to_all(known, "col", 0, 0)
    sums = segment_sums(offdiag, row_index, known.shape[0] * known.shape[1])
    within, cross = pack(plan, [after(piece, sums, known_all) for piece in line])

    got = spread(within, plan)

    keep, give = local_update(known_all, after(sums, cross), rhs, diag_inv)
    total = keep + other_core(give, plan).astype(jnp.float32)
    sent = total.astype(jnp.bfloat16)
    for m in reversed(range(1, plan.zs)):
        total = total + across_z(sent, plan, m).astype(jnp.float32)
    cross = jnp.stack([cross, other_core(cross, plan)])
    upper = after(total[plan.upper].astype(jnp.bfloat16), cross)
    values = jnp.stack(direct(upper, plan))

    got = after(got, values)
    high, low = got[:, : plan.counts[0]], got[:, plan.counts[0] :]
    high = jnp.stack([high, other_core(high, plan)])
    sizes = (NB // 2, plan.lower.stop)
    solved, lower = call_half(
        upper_kernel, plan, "upper_half", sizes, values, total[plan.lower], high, cross
    )
    values = jnp.stack(direct(lower, plan))
    low = after(low, solved)
    low = jnp.stack([low, other_core(low, plan)])
    (mine,) = call_half(
        lower_kernel, plan, "lower_half", (NB // plan.cols,), values, solved, low
    )
    mine, theirs = out_of_solvers(mine, plan)
    return jnp.concatenate(
        [jnp.where(core == 0, mine, theirs), jnp.where(core == 0, theirs, mine)], axis=1
    )


def solution(mesh):
    placed = (
        P("col", None, None),
        P("col", None, None),
        P("row", "col", None, None),
        P("row", "col", None, None),
        P(("row", "col"), None, None),
        P("row"),
    )
    return jax.shard_map(
        body, mesh=mesh, in_specs=placed, out_specs=P("col", None, None), check_vma=False
    )
```

```python
import functools

import jax
import jax.numpy as jnp
from jax import lax
from jax.experimental import pallas as pl
from jax.experimental.pallas import tpu as pltpu
from jax.sharding import PartitionSpec as P

NB = 16
AXES = ("row", "col")
VMEM_LIMIT = 16 * 1024 * 1024
HIGHEST = lax.Precision.HIGHEST


class Plan:
    def __init__(self, rows, cols):
        self.rows, self.cols, self.zs = rows, cols, rows // 2
        self.slots = [
            (a, b)
            for a in reversed(range(NB // rows))
            for b in reversed(range(NB // cols))
            if a * rows + rows - 1 > b * cols
        ]
        half = NB // 2
        self.high, self.low, self.cross = {}, {}, {}
        for core in range(2):
            for c in range(cols):
                below = [
                    (r, at, a * rows + r, b * cols + c)
                    for r in range(core, rows, 2)
                    for at, (a, b) in enumerate(self.slots)
                    if a * rows + r > b * cols + c
                ]
                self.high[core, c] = [t[:2] for t in below if t[3] >= half]
                self.low[core, c] = [t[:2] for t in below if t[2] < half]
                self.cross[core, c] = [t[:2] for t in below if t[2] >= half > t[3]]
        self.lists = (self.high, self.low, self.cross)
        self.counts = [max(map(len, lists.values())) for lists in self.lists]
        self.upper = slice(half // cols, NB // cols)
        self.lower = slice(0, -(-half // cols))
        self.solvers = sorted({max(self.zs // 2 - 1, 0), self.zs // 2})
        self.arrival = [self.zs - 1, *range(1, self.zs - 1), 0]


def send(array, plan, pairs):
    flat = [(r * plan.cols + c, to_r * plan.cols + to_c) for (r, c), (to_r, to_c) in pairs]
    return lax.ppermute(array, AXES, flat)


def across_z(array, plan, flip):
    to = {z ^ flip: z for z in plan.solvers}
    free = [z for z in range(plan.zs) if z not in to.values()]
    for z in range(plan.zs):
        if z not in to:
            to[z] = min(free, key=lambda other: abs(other - z))
            free.remove(to[z])
    pairs = [
        ((2 * z + core, c), (2 * to[z] + core, c))
        for z in range(plan.zs)
        for core in range(2)
        for c in range(plan.cols)
    ]
    return send(array, plan, pairs)


def out_of_solvers(array, plan):
    low, high = plan.solvers[0], plan.solvers[-1]
    z = lax.axis_index("row") // 2
    own, other = array, other_core(array, plan)
    for step in range(1, plan.zs // 2):
        to = {low: low - step, high: high + step, low - step: low, high + step: high}
        outer = jnp.logical_or(z == low - step, z == high + step)
        got = []
        for cross in range(2):
            pairs = [
                ((2 * a + core, c), (2 * to.get(a, a) + (core ^ cross), c))
                for a in range(plan.zs)
                for core in range(2)
                for c in range(plan.cols)
            ]
            got.append(send(array, plan, pairs))
        own, other = jnp.where(outer, got[0], own), jnp.where(outer, got[1], other)
    return own, other


def across_col(array, plan, flip):
    pairs = [((r, c), (r, c ^ flip)) for r in range(plan.rows) for c in range(plan.cols)]
    return send(array, plan, pairs)


def other_core(array, plan):
    pairs = [((r, c), (r ^ 1, c)) for r in range(plan.rows) for c in range(plan.cols)]
    return send(array, plan, pairs)


def direct(array, plan):
    return [array] + [across_col(array, plan, m) for m in range(1, plan.cols)]


NO_COST = pl.CostEstimate(flops=0, bytes_accessed=0, transcendentals=0)


def fold_kernel(slots, panel_hbm, inverse_hbm, known_hbm, out_ref, known_ref, panel_ref, inverse_ref, sems):
    copies = [
        pltpu.make_async_copy(inverse_hbm, inverse_ref, sems.at[0]),
        pltpu.make_async_copy(panel_hbm, panel_ref, sems.at[1]),
    ]
    copies += [
        pltpu.make_async_copy(known_hbm, known_ref.at[c], sems.at[2 + c])
        for c in range(known_ref.shape[0])
    ]
    for copy in copies:
        copy.start()
    for copy in copies:
        copy.wait()
    for at, (a, b) in enumerate(slots):
        inverse = inverse_ref[b]
        high = inverse.astype(jnp.bfloat16)
        low = (inverse - high.astype(jnp.float32)).astype(jnp.bfloat16)
        tile = panel_ref[a, b]
        out_ref[at] = (
            jnp.dot(tile, high, preferred_element_type=jnp.float32)
            + jnp.dot(tile, low, preferred_element_type=jnp.float32)
        ).astype(jnp.bfloat16)


def fold_panel(panel, inverse, known, slots, cols):
    bs = panel.shape[-1]
    return pl.pallas_call(
        functools.partial(fold_kernel, slots),
        in_specs=[pl.BlockSpec(memory_space=pltpu.HBM)] * 3,
        out_shape=(
            jax.ShapeDtypeStruct((len(slots), bs, bs), jnp.bfloat16),
            jax.ShapeDtypeStruct((cols, *known.shape), known.dtype),
        ),
        scratch_shapes=[
            pltpu.VMEM(panel.shape, panel.dtype),
            pltpu.VMEM(inverse.shape, inverse.dtype),
            pltpu.SemaphoreType.DMA((2 + cols,)),
        ],
        compiler_params=pltpu.CompilerParams(vmem_limit_bytes=62 * 1024 * 1024),
        cost_estimate=NO_COST,
        name="fold_panel",
    )(panel, inverse, known)


def segment_kernel(chunk, index_ref, tiles_hbm, out_ref, tiles, sums, sems):
    copies = [
        pltpu.make_async_copy(
            tiles_hbm.at[pl.ds(i * chunk, chunk)], tiles.at[pl.ds(i * chunk, chunk)], sems.at[i]
        )
        for i in range(tiles.shape[0] // chunk)
    ]
    for copy in copies:
        copy.start()
    sums[...] = jnp.zeros_like(sums)
    for i, copy in enumerate(copies):
        copy.wait()

        def add(p, carry):
            sums[index_ref[p]] += tiles[p].astype(jnp.float32)
            return carry

        lax.fori_loop(i * chunk, (i + 1) * chunk, add, 0)
    out_ref[...] = sums[...].astype(jnp.bfloat16)


def segment_sums(offdiag, row_index, segments):
    tiles, blocks, bs, _ = offdiag.shape
    chunk = 4
    return pl.pallas_call(
        functools.partial(segment_kernel, chunk),
        in_specs=[pl.BlockSpec(memory_space=pltpu.SMEM), pl.BlockSpec(memory_space=pltpu.HBM)],
        out_shape=jax.ShapeDtypeStruct((segments, blocks, bs, bs), jnp.bfloat16),
        scratch_shapes=[
            pltpu.VMEM(offdiag.shape, offdiag.dtype),
            pltpu.VMEM((segments, blocks, bs, bs), jnp.float32),
            pltpu.SemaphoreType.DMA((tiles // chunk,)),
        ],
        compiler_params=pltpu.CompilerParams(vmem_limit_bytes=52 * 1024 * 1024),
        cost_estimate=pl.CostEstimate(
            flops=offdiag.size, bytes_accessed=2 * offdiag.size, transcendentals=0
        ),
        name="segment_sums",
    )(row_index, offdiag)


def update_kernel(known_ref, sums_ref, rhs_ref, inverse_ref, keep_ref, give_ref, whole):
    blocks, count, bs = rhs_ref.shape
    cols, per = known_ref.shape[:2]
    row_id = lax.axis_index("row")
    off = [jnp.zeros((count, bs), jnp.float32)] * blocks
    for c in range(cols):
        for i in range(per):
            for b in range(blocks):
                off[b] += jnp.dot(
                    known_ref[c, i], sums_ref[c * per + i, b], preferred_element_type=jnp.float32
                )
    adds = (row_id == 0).astype(jnp.float32)
    for b in range(blocks):
        total = rhs_ref[b] * adds - off[b]
        whole[b] = jnp.dot(
            total, inverse_ref[b], precision=HIGHEST, preferred_element_type=jnp.float32
        )
    half = count // 2
    core = lax.rem(row_id, 2)
    keep = pl.ds(pl.multiple_of(core * half, half), half)
    give = pl.ds(pl.multiple_of((1 - core) * half, half), half)
    keep_ref[...] = whole[:, keep, :]
    give_ref[...] = whole[:, give, :].astype(jnp.bfloat16)


def local_update(known, sums, rhs, inverse):
    blocks, count, bs = rhs.shape
    half = (blocks, count // 2, bs)
    return pl.pallas_call(
        update_kernel,
        out_shape=(
            jax.ShapeDtypeStruct(half, jnp.float32),
            jax.ShapeDtypeStruct(half, jnp.bfloat16),
        ),
        scratch_shapes=[pltpu.VMEM(rhs.shape, jnp.float32)],
        compiler_params=pltpu.CompilerParams(vmem_limit_bytes=VMEM_LIMIT),
        cost_estimate=NO_COST,
        name="local_update",
    )(known, sums, rhs, inverse)


def pack_kernel(plan, *refs):
    line_refs = [refs[plan.arrival.index(step)] for step in range(plan.zs)]
    row_id, col_id = lax.axis_index("row"), lax.axis_index("col")
    core, z = lax.rem(row_id, 2), row_id // 2
    within_ref, cross_ref = refs[plan.zs :]
    for which, (lists, count) in enumerate(zip(plan.lists, plan.counts)):
        out_ref = cross_ref if which == 2 else within_ref
        first = plan.counts[0] if which == 1 else 0
        for i in range(count):
            back, at = jnp.int32(0), jnp.int32(0)
            for (side, c), found in lists.items():
                if i < len(found):
                    mine = jnp.logical_and(col_id == c, core == side)
                    back = jnp.where(mine, lax.bitwise_xor(z, found[i][0] // 2), back)
                    at = jnp.where(mine, found[i][1], at)
            for step, line_ref in enumerate(line_refs):

                @pl.when(back == step)
                def _():
                    out_ref[first + i] = line_ref[at]


def pack(plan, line):
    bs = line[0].shape[-1]
    return pl.pallas_call(
        functools.partial(pack_kernel, plan),
        out_shape=[
            jax.ShapeDtypeStruct((count, bs, bs), jnp.bfloat16)
            for count in (sum(plan.counts[:2]), plan.counts[2])
        ],
        compiler_params=pltpu.CompilerParams(vmem_limit_bytes=VMEM_LIMIT),
        cost_estimate=NO_COST,
        name="pack",
    )(*[line[step] for step in plan.arrival])


def solve(plan, value_ref, tiles_ref, values, solved, first):
    rows, cols, half = plan.rows, plan.cols, NB // 2
    core, col_id = lax.rem(lax.axis_index("row"), 2), lax.axis_index("col")
    for step in range(cols):
        owner = lax.bitwise_xor(col_id, step)
        for b in range(value_ref.shape[1]):
            values[b * cols + owner] = value_ref[step, b].astype(jnp.float32)

    def tile(j, k):
        r, c = j % rows, k % cols
        lists = plan.high if first else plan.low
        at = lists[r % 2, c].index((r, plan.slots.index((j // rows, k // cols))))
        return tiles_ref[lax.bitwise_xor(core, r % 2), lax.bitwise_xor(col_id, c), at]

    skip = first // cols * cols
    sums = [values[first - skip + i] for i in range(half)]
    for i in reversed(range(half)):
        block = sums[i].astype(jnp.bfloat16)
        solved[first + i] = block
        for m in reversed(range(i)):
            sums[m] = sums[m] - jnp.dot(
                block, tile(first + i, first + m), preferred_element_type=jnp.float32
            )


def upper_kernel(plan, value_ref, own_ref, tiles_ref, cross_ref, out_ref, lower_ref, values, solved):
    rows, half = plan.rows, NB // 2
    core = lax.rem(lax.axis_index("row"), 2)
    solve(plan, value_ref, tiles_ref, values, solved, half)
    out_ref[...] = solved[pl.ds(half, half)]
    for b in range(own_ref.shape[0]):
        total = own_ref[b]
        for j in range(half, NB):
            r = j % rows
            at = plan.cross[r % 2, 0].index((r, plan.slots.index((j // rows, b))))
            tile = cross_ref[lax.bitwise_xor(core, r % 2), at]
            total = total - jnp.dot(solved[j], tile, preferred_element_type=jnp.float32)
        lower_ref[b] = total.astype(jnp.bfloat16)


def lower_kernel(plan, value_ref, upper_ref, tiles_ref, out_ref, values, solved):
    half, col_id = NB // 2, lax.axis_index("col")
    solved[pl.ds(half, half)] = upper_ref[...]
    solve(plan, value_ref, tiles_ref, values, solved, 0)
    for b in range(out_ref.shape[0]):
        out_ref[b] = solved[b * plan.cols + col_id]


def call_half(kernel, plan, name, out_shape, values, *args):
    _, blocks, count, bs = values.shape
    return pl.pallas_call(
        functools.partial(kernel, plan),
        out_shape=[jax.ShapeDtypeStruct((n, count, bs), jnp.bfloat16) for n in out_shape],
        scratch_shapes=[
            pltpu.VMEM((blocks * plan.cols, count, bs), jnp.float32),
            pltpu.VMEM((NB, count, bs), jnp.bfloat16),
        ],
        compiler_params=pltpu.CompilerParams(vmem_limit_bytes=VMEM_LIMIT),
        cost_estimate=NO_COST,
        name=name,
    )(values, *args)


def after(array, *done):
    return lax.optimization_barrier((array, *done))[0]


def body(rhs, diag_inv, panel, offdiag, known, row_index):
    plan = Plan(lax.axis_size("row"), lax.axis_size("col"))
    core = lax.rem(lax.axis_index("row"), 2)

    folded, known = fold_panel(panel, diag_inv, known, plan.slots, plan.cols)
    line = [folded] + [across_z(folded, plan, m) for m in range(1, plan.zs)]
    known_all = lax.all_to_all(known, "col", 0, 0)
    sums = segment_sums(offdiag, row_index, known.shape[0] * known.shape[1])
    within, cross = pack(plan, [after(piece, sums, known_all) for piece in line])

    got = direct(within, plan)

    keep, give = local_update(known_all, after(sums, cross), rhs, diag_inv)
    total = keep + other_core(give, plan).astype(jnp.float32)
    sent = total.astype(jnp.bfloat16)
    for m in range(1, plan.zs // 2):
        total = total + across_z(sent, plan, m).astype(jnp.float32)
    sent = total.astype(jnp.bfloat16)
    total = total + across_z(sent, plan, plan.zs - 1).astype(jnp.float32)
    cross = jnp.stack([cross, other_core(cross, plan)])
    upper = after(total[plan.upper].astype(jnp.bfloat16), cross, got[1], got[2 % plan.cols])
    values = jnp.stack(direct(upper, plan))

    split = plan.counts[0]
    early, late = jnp.stack(got[:-1]), after(got[-1], values)[None]
    high = [jnp.concatenate([early[:, :split], late[:, :split]])]
    high.append(
        jnp.concatenate([other_core(piece[:, :split], plan) for piece in (early, late)])
    )
    high = jnp.stack(high)
    low = jnp.concatenate([early[:, split:], late[:, split:]])
    sizes = (NB // 2, plan.lower.stop)
    solved, lower = call_half(
        upper_kernel, plan, "upper_half", sizes, values, total[plan.lower], high, cross
    )
    values = jnp.stack(direct(lower, plan))
    low = after(low, solved)
    low = jnp.stack([low, other_core(low, plan)])
    (mine,) = call_half(
        lower_kernel, plan, "lower_half", (NB // plan.cols,), values, solved, low
    )
    mine, theirs = out_of_solvers(mine, plan)
    return jnp.concatenate(
        [jnp.where(core == 0, mine, theirs), jnp.where(core == 0, theirs, mine)], axis=1
    )


def solution(mesh):
    placed = (
        P("col", None, None),
        P("col", None, None),
        P("row", "col", None, None),
        P("row", "col", None, None),
        P(("row", "col"), None, None),
        P("row"),
    )
    return jax.shard_map(
        body, mesh=mesh, in_specs=placed, out_specs=P("col", None, None), check_vma=False
    )
```

```python
import functools

import jax
import jax.numpy as jnp
from jax import lax
from jax.experimental import pallas as pl
from jax.experimental.pallas import tpu as pltpu
from jax.sharding import PartitionSpec as P

NB = 16
AXES = ("row", "col")
VMEM_LIMIT = 16 * 1024 * 1024
HIGHEST = lax.Precision.HIGHEST


class Plan:
    def __init__(self, rows, cols):
        self.rows, self.cols, self.zs = rows, cols, rows // 2
        self.slots = [
            (a, b)
            for a in reversed(range(NB // rows))
            for b in reversed(range(NB // cols))
            if a * rows + rows - 1 > b * cols
        ]
        half = NB // 2
        self.high, self.low, self.cross = {}, {}, {}
        for core in range(2):
            for c in range(cols):
                below = [
                    (r, at, a * rows + r, b * cols + c)
                    for r in range(core, rows, 2)
                    for at, (a, b) in enumerate(self.slots)
                    if a * rows + r > b * cols + c
                ]
                self.high[core, c] = [t[:2] for t in below if t[3] >= half]
                self.low[core, c] = [t[:2] for t in below if t[2] < half]
                self.cross[core, c] = [t[:2] for t in below if t[2] >= half > t[3]]
        self.lists = (self.high, self.low, self.cross)
        self.counts = [max(map(len, lists.values())) for lists in self.lists]
        self.upper = slice(half // cols, NB // cols)
        self.lower = slice(0, -(-half // cols))
        self.solvers = sorted({max(self.zs // 2 - 1, 0), self.zs // 2})
        self.arrival = [self.zs - 1, *range(1, self.zs - 1), 0]


def send(array, plan, pairs):
    flat = [(r * plan.cols + c, to_r * plan.cols + to_c) for (r, c), (to_r, to_c) in pairs]
    return lax.ppermute(array, AXES, flat)


def across_z(array, plan, flip):
    to = {z ^ flip: z for z in plan.solvers}
    free = [z for z in range(plan.zs) if z not in to.values()]
    for z in range(plan.zs):
        if z not in to:
            to[z] = min(free, key=lambda other: abs(other - z))
            free.remove(to[z])
    pairs = [
        ((2 * z + core, c), (2 * to[z] + core, c))
        for z in range(plan.zs)
        for core in range(2)
        for c in range(plan.cols)
    ]
    return send(array, plan, pairs)


def out_of_solvers(array, plan):
    low, high = plan.solvers[0], plan.solvers[-1]
    z = lax.axis_index("row") // 2
    own, other = array, other_core(array, plan)
    for step in range(1, plan.zs // 2):
        to = {low: low - step, high: high + step, low - step: low, high + step: high}
        outer = jnp.logical_or(z == low - step, z == high + step)
        got = []
        for cross in range(2):
            pairs = [
                ((2 * a + core, c), (2 * to.get(a, a) + (core ^ cross), c))
                for a in range(plan.zs)
                for core in range(2)
                for c in range(plan.cols)
            ]
            got.append(send(array, plan, pairs))
        own, other = jnp.where(outer, got[0], own), jnp.where(outer, got[1], other)
    return own, other


def across_col(array, plan, flip):
    pairs = [((r, c), (r, c ^ flip)) for r in range(plan.rows) for c in range(plan.cols)]
    return send(array, plan, pairs)


def other_core(array, plan):
    pairs = [((r, c), (r ^ 1, c)) for r in range(plan.rows) for c in range(plan.cols)]
    return send(array, plan, pairs)


def direct(array, plan):
    return [array] + [across_col(array, plan, m) for m in range(1, plan.cols)]


NO_COST = pl.CostEstimate(flops=0, bytes_accessed=0, transcendentals=0)


def fold_kernel(slots, panel_hbm, inverse_hbm, known_hbm, out_ref, known_ref, panel_ref, inverse_ref, sems):
    copies = [
        pltpu.make_async_copy(inverse_hbm, inverse_ref, sems.at[0]),
        pltpu.make_async_copy(panel_hbm, panel_ref, sems.at[1]),
    ]
    copies += [
        pltpu.make_async_copy(known_hbm, known_ref.at[c], sems.at[2 + c])
        for c in range(known_ref.shape[0])
    ]
    for copy in copies:
        copy.start()
    for copy in copies:
        copy.wait()
    for at, (a, b) in enumerate(slots):
        inverse = inverse_ref[b]
        high = inverse.astype(jnp.bfloat16)
        low = (inverse - high.astype(jnp.float32)).astype(jnp.bfloat16)
        tile = panel_ref[a, b]
        out_ref[at] = (
            jnp.dot(tile, high, preferred_element_type=jnp.float32)
            + jnp.dot(tile, low, preferred_element_type=jnp.float32)
        ).astype(jnp.bfloat16)


def fold_panel(panel, inverse, known, slots, cols):
    bs = panel.shape[-1]
    return pl.pallas_call(
        functools.partial(fold_kernel, slots),
        in_specs=[pl.BlockSpec(memory_space=pltpu.HBM)] * 3,
        out_shape=(
            jax.ShapeDtypeStruct((len(slots), bs, bs), jnp.bfloat16),
            jax.ShapeDtypeStruct((cols, *known.shape), known.dtype),
        ),
        scratch_shapes=[
            pltpu.VMEM(panel.shape, panel.dtype),
            pltpu.VMEM(inverse.shape, inverse.dtype),
            pltpu.SemaphoreType.DMA((2 + cols,)),
        ],
        compiler_params=pltpu.CompilerParams(vmem_limit_bytes=62 * 1024 * 1024),
        cost_estimate=NO_COST,
        name="fold_panel",
    )(panel, inverse, known)


def segment_kernel(chunk, index_ref, tiles_hbm, out_ref, tiles, sums, sems):
    copies = [
        pltpu.make_async_copy(
            tiles_hbm.at[pl.ds(i * chunk, chunk)], tiles.at[pl.ds(i * chunk, chunk)], sems.at[i]
        )
        for i in range(tiles.shape[0] // chunk)
    ]
    for copy in copies:
        copy.start()
    sums[...] = jnp.zeros_like(sums)
    for i, copy in enumerate(copies):
        copy.wait()

        def add(p, carry):
            sums[index_ref[p]] += tiles[p].astype(jnp.float32)
            return carry

        lax.fori_loop(i * chunk, (i + 1) * chunk, add, 0)
    out_ref[...] = sums[...].astype(jnp.bfloat16)


def segment_sums(offdiag, row_index, segments):
    tiles, blocks, bs, _ = offdiag.shape
    chunk = 4
    return pl.pallas_call(
        functools.partial(segment_kernel, chunk),
        in_specs=[pl.BlockSpec(memory_space=pltpu.SMEM), pl.BlockSpec(memory_space=pltpu.HBM)],
        out_shape=jax.ShapeDtypeStruct((segments, blocks, bs, bs), jnp.bfloat16),
        scratch_shapes=[
            pltpu.VMEM(offdiag.shape, offdiag.dtype),
            pltpu.VMEM((segments, blocks, bs, bs), jnp.float32),
            pltpu.SemaphoreType.DMA((tiles // chunk,)),
        ],
        compiler_params=pltpu.CompilerParams(vmem_limit_bytes=52 * 1024 * 1024),
        cost_estimate=pl.CostEstimate(
            flops=offdiag.size, bytes_accessed=2 * offdiag.size, transcendentals=0
        ),
        name="segment_sums",
    )(row_index, offdiag)


def update_kernel(known_ref, sums_ref, rhs_ref, inverse_ref, keep_ref, give_ref, whole):
    blocks, count, bs = rhs_ref.shape
    cols, per = known_ref.shape[:2]
    row_id = lax.axis_index("row")
    off = [jnp.zeros((count, bs), jnp.float32)] * blocks
    for c in range(cols):
        for i in range(per):
            for b in range(blocks):
                off[b] += jnp.dot(
                    known_ref[c, i], sums_ref[c * per + i, b], preferred_element_type=jnp.float32
                )
    adds = (row_id == 0).astype(jnp.float32)
    for b in range(blocks):
        total = rhs_ref[b] * adds - off[b]
        whole[b] = jnp.dot(
            total, inverse_ref[b], precision=HIGHEST, preferred_element_type=jnp.float32
        )
    half = count // 2
    core = lax.rem(row_id, 2)
    keep = pl.ds(pl.multiple_of(core * half, half), half)
    give = pl.ds(pl.multiple_of((1 - core) * half, half), half)
    keep_ref[...] = whole[:, keep, :]
    give_ref[...] = whole[:, give, :].astype(jnp.bfloat16)


def local_update(known, sums, rhs, inverse):
    blocks, count, bs = rhs.shape
    half = (blocks, count // 2, bs)
    return pl.pallas_call(
        update_kernel,
        out_shape=(
            jax.ShapeDtypeStruct(half, jnp.float32),
            jax.ShapeDtypeStruct(half, jnp.bfloat16),
        ),
        scratch_shapes=[pltpu.VMEM(rhs.shape, jnp.float32)],
        compiler_params=pltpu.CompilerParams(vmem_limit_bytes=VMEM_LIMIT),
        cost_estimate=NO_COST,
        name="local_update",
    )(known, sums, rhs, inverse)


def pack_kernel(plan, *refs):
    line_refs = [refs[plan.arrival.index(step)] for step in range(plan.zs)]
    row_id, col_id = lax.axis_index("row"), lax.axis_index("col")
    core, z = lax.rem(row_id, 2), row_id // 2
    within_ref, cross_ref = refs[plan.zs :]
    for which, (lists, count) in enumerate(zip(plan.lists, plan.counts)):
        out_ref = cross_ref if which == 2 else within_ref
        first = plan.counts[0] if which == 1 else 0
        for i in range(count):
            back, at = jnp.int32(0), jnp.int32(0)
            for (side, c), found in lists.items():
                if i < len(found):
                    mine = jnp.logical_and(col_id == c, core == side)
                    back = jnp.where(mine, lax.bitwise_xor(z, found[i][0] // 2), back)
                    at = jnp.where(mine, found[i][1], at)
            for step, line_ref in enumerate(line_refs):

                @pl.when(back == step)
                def _():
                    out_ref[first + i] = line_ref[at]


def pack(plan, line):
    bs = line[0].shape[-1]
    return pl.pallas_call(
        functools.partial(pack_kernel, plan),
        out_shape=[
            jax.ShapeDtypeStruct((count, bs, bs), jnp.bfloat16)
            for count in (sum(plan.counts[:2]), plan.counts[2])
        ],
        compiler_params=pltpu.CompilerParams(vmem_limit_bytes=VMEM_LIMIT),
        cost_estimate=NO_COST,
        name="pack",
    )(*[line[step] for step in plan.arrival])


def solve(plan, value_ref, tiles_ref, values, solved, first):
    rows, cols, half = plan.rows, plan.cols, NB // 2
    core, col_id = lax.rem(lax.axis_index("row"), 2), lax.axis_index("col")
    for step in range(cols):
        owner = lax.bitwise_xor(col_id, step)
        for b in range(value_ref.shape[1]):
            values[b * cols + owner] = value_ref[step, b].astype(jnp.float32)

    def tile(j, k):
        r, c = j % rows, k % cols
        lists = plan.high if first else plan.low
        at = lists[r % 2, c].index((r, plan.slots.index((j // rows, k // cols))))
        return tiles_ref[lax.bitwise_xor(core, r % 2), lax.bitwise_xor(col_id, c), at]

    skip = first // cols * cols
    sums = [values[first - skip + i] for i in range(half)]
    for i in reversed(range(half)):
        block = sums[i].astype(jnp.bfloat16)
        solved[first + i] = block
        for m in reversed(range(i)):
            sums[m] = sums[m] - jnp.dot(
                block, tile(first + i, first + m), preferred_element_type=jnp.float32
            )


def upper_kernel(plan, value_ref, own_ref, tiles_ref, cross_ref, out_ref, lower_ref, values, solved):
    rows, half = plan.rows, NB // 2
    core = lax.rem(lax.axis_index("row"), 2)
    solve(plan, value_ref, tiles_ref, values, solved, half)
    out_ref[...] = solved[pl.ds(half, half)]
    for b in range(own_ref.shape[0]):
        total = own_ref[b]
        for j in range(half, NB):
            r = j % rows
            at = plan.cross[r % 2, 0].index((r, plan.slots.index((j // rows, b))))
            tile = cross_ref[lax.bitwise_xor(core, r % 2), at]
            total = total - jnp.dot(solved[j], tile, preferred_element_type=jnp.float32)
        lower_ref[b] = total.astype(jnp.bfloat16)


def lower_kernel(plan, value_ref, upper_ref, tiles_ref, out_ref, values, solved):
    half, col_id = NB // 2, lax.axis_index("col")
    solved[pl.ds(half, half)] = upper_ref[...]
    solve(plan, value_ref, tiles_ref, values, solved, 0)
    for b in range(out_ref.shape[0]):
        out_ref[b] = solved[b * plan.cols + col_id]


def call_half(kernel, plan, name, out_shape, values, *args):
    _, blocks, count, bs = values.shape
    return pl.pallas_call(
        functools.partial(kernel, plan),
        out_shape=[jax.ShapeDtypeStruct((n, count, bs), jnp.bfloat16) for n in out_shape],
        scratch_shapes=[
            pltpu.VMEM((blocks * plan.cols, count, bs), jnp.float32),
            pltpu.VMEM((NB, count, bs), jnp.bfloat16),
        ],
        compiler_params=pltpu.CompilerParams(vmem_limit_bytes=VMEM_LIMIT),
        cost_estimate=NO_COST,
        name=name,
    )(values, *args)


def after(array, *done):
    return lax.optimization_barrier((array, *done))[0]


def body(rhs, diag_inv, panel, offdiag, known, row_index):
    plan = Plan(lax.axis_size("row"), lax.axis_size("col"))
    core = lax.rem(lax.axis_index("row"), 2)

    folded, known = fold_panel(panel, diag_inv, known, plan.slots, plan.cols)
    line = [folded] + [across_z(folded, plan, m) for m in range(1, plan.zs)]
    known_all = lax.all_to_all(known, "col", 0, 0)
    sums = segment_sums(offdiag, row_index, known.shape[0] * known.shape[1])
    within, cross = pack(plan, [after(piece, sums, known_all) for piece in line])

    got = direct(within, plan)

    keep, give = local_update(known_all, after(sums, cross), rhs, diag_inv)
    total = keep + other_core(give, plan).astype(jnp.float32)
    sent = total.astype(jnp.bfloat16)
    for m in range(1, plan.zs // 2):
        total = total + across_z(sent, plan, m).astype(jnp.float32)
    sent = total.astype(jnp.bfloat16)
    total = total + across_z(sent, plan, plan.zs - 1).astype(jnp.float32)
    cross = jnp.stack([cross, other_core(cross, plan)])
    upper = after(total[plan.upper].astype(jnp.bfloat16), cross, got[1])
    values = jnp.stack(direct(upper, plan))

    split = plan.counts[0]
    early, late = jnp.stack(got[:-1]), got[-1][None]
    high = [jnp.concatenate([early[:, :split], late[:, :split]])]
    high.append(
        jnp.concatenate([other_core(piece[:, :split], plan) for piece in (early, late)])
    )
    high = jnp.stack(high)
    low = jnp.concatenate([early[:, split:], late[:, split:]])
    sizes = (NB // 2, plan.lower.stop)
    solved, lower = call_half(
        upper_kernel, plan, "upper_half", sizes, values, total[plan.lower], high, cross
    )
    values = jnp.stack(direct(lower, plan))
    low = after(low, solved)
    low = jnp.stack([low, other_core(low, plan)])
    (mine,) = call_half(
        lower_kernel, plan, "lower_half", (NB // plan.cols,), values, solved, low
    )
    mine, theirs = out_of_solvers(mine, plan)
    return jnp.concatenate(
        [jnp.where(core == 0, mine, theirs), jnp.where(core == 0, theirs, mine)], axis=1
    )


def solution(mesh):
    placed = (
        P("col", None, None),
        P("col", None, None),
        P("row", "col", None, None),
        P("row", "col", None, None),
        P(("row", "col"), None, None),
        P("row"),
    )
    return jax.shard_map(
        body, mesh=mesh, in_specs=placed, out_specs=P("col", None, None), check_vma=False
    )
```

```python
import functools

import jax
import jax.numpy as jnp
from jax import lax
from jax.experimental import pallas as pl
from jax.experimental.pallas import tpu as pltpu
from jax.sharding import PartitionSpec as P

NB = 16
AXES = ("row", "col")
VMEM_LIMIT = 16 * 1024 * 1024
HIGHEST = lax.Precision.HIGHEST


class Plan:
    def __init__(self, rows, cols):
        self.rows, self.cols, self.zs = rows, cols, rows // 2
        self.slots = [
            (a, b)
            for a in reversed(range(NB // rows))
            for b in reversed(range(NB // cols))
            if a * rows + rows - 1 > b * cols
        ]
        half = NB // 2
        self.high, self.low, self.cross = {}, {}, {}
        for core in range(2):
            for c in range(cols):
                below = [
                    (r, at, a * rows + r, b * cols + c)
                    for r in range(core, rows, 2)
                    for at, (a, b) in enumerate(self.slots)
                    if a * rows + r > b * cols + c
                ]
                self.high[core, c] = [t[:2] for t in below if t[3] >= half]
                self.low[core, c] = [t[:2] for t in below if t[2] < half]
                self.cross[core, c] = [t[:2] for t in below if t[2] >= half > t[3]]
        self.lists = (self.high, self.low, self.cross)
        self.counts = [max(map(len, lists.values())) for lists in self.lists]
        self.upper = slice(half // cols, NB // cols)
        self.lower = slice(0, -(-half // cols))
        self.solvers = sorted({max(self.zs // 2 - 1, 0), self.zs // 2})
        self.arrival = [self.zs - 1, *range(1, self.zs - 1), 0]


def send(array, plan, pairs):
    flat = [(r * plan.cols + c, to_r * plan.cols + to_c) for (r, c), (to_r, to_c) in pairs]
    return lax.ppermute(array, AXES, flat)


def across_z(array, plan, flip):
    to = {z ^ flip: z for z in plan.solvers}
    free = [z for z in range(plan.zs) if z not in to.values()]
    for z in range(plan.zs):
        if z not in to:
            to[z] = min(free, key=lambda other: abs(other - z))
            free.remove(to[z])
    pairs = [
        ((2 * z + core, c), (2 * to[z] + core, c))
        for z in range(plan.zs)
        for core in range(2)
        for c in range(plan.cols)
    ]
    return send(array, plan, pairs)


def out_of_solvers(array, plan):
    low, high = plan.solvers[0], plan.solvers[-1]
    z = lax.axis_index("row") // 2
    own, other = array, other_core(array, plan)
    for step in range(1, plan.zs // 2):
        to = {low: low - step, high: high + step, low - step: low, high + step: high}
        outer = jnp.logical_or(z == low - step, z == high + step)
        got = []
        for cross in range(2):
            pairs = [
                ((2 * a + core, c), (2 * to.get(a, a) + (core ^ cross), c))
                for a in range(plan.zs)
                for core in range(2)
                for c in range(plan.cols)
            ]
            got.append(send(array, plan, pairs))
        own, other = jnp.where(outer, got[0], own), jnp.where(outer, got[1], other)
    return own, other


def across_col(array, plan, flip):
    pairs = [((r, c), (r, c ^ flip)) for r in range(plan.rows) for c in range(plan.cols)]
    return send(array, plan, pairs)


def other_core(array, plan):
    pairs = [((r, c), (r ^ 1, c)) for r in range(plan.rows) for c in range(plan.cols)]
    return send(array, plan, pairs)


def direct(array, plan):
    return [array] + [across_col(array, plan, m) for m in range(1, plan.cols)]


NO_COST = pl.CostEstimate(flops=0, bytes_accessed=0, transcendentals=0)


def fold_kernel(slots, panel_hbm, inverse_hbm, known_hbm, out_ref, known_ref, panel_ref, inverse_ref, sems):
    blocks, cols = inverse_ref.shape[0], known_ref.shape[0]
    pairs = [(inverse_hbm.at[b], inverse_ref.at[b]) for b in range(blocks)]
    pairs += [(panel_hbm.at[a, b], panel_ref.at[at]) for at, (a, b) in enumerate(slots)]
    pairs += [(known_hbm, known_ref.at[c]) for c in range(cols)]
    copies = [pltpu.make_async_copy(x, y, sems.at[i]) for i, (x, y) in enumerate(pairs)]
    for copy in copies:
        copy.start()
    for copy in copies[:blocks]:
        copy.wait()
    for at, (_, b) in enumerate(slots):
        copies[blocks + at].wait()
        inverse = inverse_ref[b]
        high = inverse.astype(jnp.bfloat16)
        low = (inverse - high.astype(jnp.float32)).astype(jnp.bfloat16)
        tile = panel_ref[at]
        out_ref[at] = (
            jnp.dot(tile, high, preferred_element_type=jnp.float32)
            + jnp.dot(tile, low, preferred_element_type=jnp.float32)
        ).astype(jnp.bfloat16)
    for copy in copies[blocks + len(slots) :]:
        copy.wait()


def fold_panel(panel, inverse, known, slots, cols):
    bs = panel.shape[-1]
    return pl.pallas_call(
        functools.partial(fold_kernel, slots),
        in_specs=[pl.BlockSpec(memory_space=pltpu.HBM)] * 3,
        out_shape=(
            jax.ShapeDtypeStruct((len(slots), bs, bs), jnp.bfloat16),
            jax.ShapeDtypeStruct((cols, *known.shape), known.dtype),
        ),
        scratch_shapes=[
            pltpu.VMEM((len(slots), bs, bs), panel.dtype),
            pltpu.VMEM(inverse.shape, inverse.dtype),
            pltpu.SemaphoreType.DMA((inverse.shape[0] + len(slots) + cols,)),
        ],
        compiler_params=pltpu.CompilerParams(vmem_limit_bytes=62 * 1024 * 1024),
        cost_estimate=NO_COST,
        name="fold_panel",
    )(panel, inverse, known)


def segment_kernel(chunk, index_ref, tiles_hbm, out_ref, tiles, sums, sems):
    copies = [
        pltpu.make_async_copy(
            tiles_hbm.at[pl.ds(i * chunk, chunk)], tiles.at[pl.ds(i * chunk, chunk)], sems.at[i]
        )
        for i in range(tiles.shape[0] // chunk)
    ]
    for copy in copies:
        copy.start()
    sums[...] = jnp.zeros_like(sums)
    for i, copy in enumerate(copies):
        copy.wait()

        def add(p, carry):
            sums[index_ref[p]] += tiles[p].astype(jnp.float32)
            return carry

        lax.fori_loop(i * chunk, (i + 1) * chunk, add, 0)
    out_ref[...] = sums[...].astype(jnp.bfloat16)


def segment_sums(offdiag, row_index, segments):
    tiles, blocks, bs, _ = offdiag.shape
    chunk = 4
    return pl.pallas_call(
        functools.partial(segment_kernel, chunk),
        in_specs=[pl.BlockSpec(memory_space=pltpu.SMEM), pl.BlockSpec(memory_space=pltpu.HBM)],
        out_shape=jax.ShapeDtypeStruct((segments, blocks, bs, bs), jnp.bfloat16),
        scratch_shapes=[
            pltpu.VMEM(offdiag.shape, offdiag.dtype),
            pltpu.VMEM((segments, blocks, bs, bs), jnp.float32),
            pltpu.SemaphoreType.DMA((tiles // chunk,)),
        ],
        compiler_params=pltpu.CompilerParams(vmem_limit_bytes=52 * 1024 * 1024),
        cost_estimate=pl.CostEstimate(
            flops=offdiag.size, bytes_accessed=2 * offdiag.size, transcendentals=0
        ),
        name="segment_sums",
    )(row_index, offdiag)


def update_kernel(known_ref, sums_ref, rhs_ref, inverse_ref, keep_ref, give_ref, whole):
    blocks, count, bs = rhs_ref.shape
    cols, per = known_ref.shape[:2]
    row_id = lax.axis_index("row")
    off = [jnp.zeros((count, bs), jnp.float32)] * blocks
    for c in range(cols):
        for i in range(per):
            for b in range(blocks):
                off[b] += jnp.dot(
                    known_ref[c, i], sums_ref[c * per + i, b], preferred_element_type=jnp.float32
                )
    adds = (row_id == 0).astype(jnp.float32)
    for b in range(blocks):
        total = rhs_ref[b] * adds - off[b]
        whole[b] = jnp.dot(
            total, inverse_ref[b], precision=HIGHEST, preferred_element_type=jnp.float32
        )
    half = count // 2
    core = lax.rem(row_id, 2)
    keep = pl.ds(pl.multiple_of(core * half, half), half)
    give = pl.ds(pl.multiple_of((1 - core) * half, half), half)
    keep_ref[...] = whole[:, keep, :]
    give_ref[...] = whole[:, give, :].astype(jnp.bfloat16)


def local_update(known, sums, rhs, inverse):
    blocks, count, bs = rhs.shape
    half = (blocks, count // 2, bs)
    return pl.pallas_call(
        update_kernel,
        out_shape=(
            jax.ShapeDtypeStruct(half, jnp.float32),
            jax.ShapeDtypeStruct(half, jnp.bfloat16),
        ),
        scratch_shapes=[pltpu.VMEM(rhs.shape, jnp.float32)],
        compiler_params=pltpu.CompilerParams(vmem_limit_bytes=VMEM_LIMIT),
        cost_estimate=NO_COST,
        name="local_update",
    )(known, sums, rhs, inverse)


def pack_kernel(plan, *refs):
    line_refs = [refs[plan.arrival.index(step)] for step in range(plan.zs)]
    row_id, col_id = lax.axis_index("row"), lax.axis_index("col")
    core, z = lax.rem(row_id, 2), row_id // 2
    within_ref, cross_ref = refs[plan.zs :]
    for which, (lists, count) in enumerate(zip(plan.lists, plan.counts)):
        out_ref = cross_ref if which == 2 else within_ref
        first = plan.counts[0] if which == 1 else 0
        for i in range(count):
            back, at = jnp.int32(0), jnp.int32(0)
            for (side, c), found in lists.items():
                if i < len(found):
                    mine = jnp.logical_and(col_id == c, core == side)
                    back = jnp.where(mine, lax.bitwise_xor(z, found[i][0] // 2), back)
                    at = jnp.where(mine, found[i][1], at)
            for step, line_ref in enumerate(line_refs):

                @pl.when(back == step)
                def _():
                    out_ref[first + i] = line_ref[at]


def pack(plan, line):
    bs = line[0].shape[-1]
    return pl.pallas_call(
        functools.partial(pack_kernel, plan),
        out_shape=[
            jax.ShapeDtypeStruct((count, bs, bs), jnp.bfloat16)
            for count in (sum(plan.counts[:2]), plan.counts[2])
        ],
        compiler_params=pltpu.CompilerParams(vmem_limit_bytes=VMEM_LIMIT),
        cost_estimate=NO_COST,
        name="pack",
    )(*[line[step] for step in plan.arrival])


def solve(plan, value_ref, tiles_ref, values, solved, first):
    rows, cols, half = plan.rows, plan.cols, NB // 2
    core, col_id = lax.rem(lax.axis_index("row"), 2), lax.axis_index("col")
    for step in range(cols):
        owner = lax.bitwise_xor(col_id, step)
        for b in range(value_ref.shape[1]):
            values[b * cols + owner] = value_ref[step, b].astype(jnp.float32)

    def tile(j, k):
        r, c = j % rows, k % cols
        lists = plan.high if first else plan.low
        at = lists[r % 2, c].index((r, plan.slots.index((j // rows, k // cols))))
        return tiles_ref[lax.bitwise_xor(core, r % 2), lax.bitwise_xor(col_id, c), at]

    skip = first // cols * cols
    sums = [values[first - skip + i] for i in range(half)]
    for i in reversed(range(half)):
        block = sums[i].astype(jnp.bfloat16)
        solved[first + i] = block
        for m in reversed(range(i)):
            sums[m] = sums[m] - jnp.dot(
                block, tile(first + i, first + m), preferred_element_type=jnp.float32
            )


def upper_kernel(plan, value_ref, own_ref, tiles_ref, cross_ref, out_ref, lower_ref, values, solved):
    rows, half = plan.rows, NB // 2
    core = lax.rem(lax.axis_index("row"), 2)
    solve(plan, value_ref, tiles_ref, values, solved, half)
    out_ref[...] = solved[pl.ds(half, half)]
    for b in range(own_ref.shape[0]):
        total = own_ref[b]
        for j in range(half, NB):
            r = j % rows
            at = plan.cross[r % 2, 0].index((r, plan.slots.index((j // rows, b))))
            tile = cross_ref[lax.bitwise_xor(core, r % 2), at]
            total = total - jnp.dot(solved[j], tile, preferred_element_type=jnp.float32)
        lower_ref[b] = total.astype(jnp.bfloat16)


def lower_kernel(plan, value_ref, upper_ref, tiles_ref, out_ref, values, solved):
    half, col_id = NB // 2, lax.axis_index("col")
    solved[pl.ds(half, half)] = upper_ref[...]
    solve(plan, value_ref, tiles_ref, values, solved, 0)
    for b in range(out_ref.shape[0]):
        out_ref[b] = solved[b * plan.cols + col_id]


def call_half(kernel, plan, name, out_shape, values, *args):
    _, blocks, count, bs = values.shape
    return pl.pallas_call(
        functools.partial(kernel, plan),
        out_shape=[jax.ShapeDtypeStruct((n, count, bs), jnp.bfloat16) for n in out_shape],
        scratch_shapes=[
            pltpu.VMEM((blocks * plan.cols, count, bs), jnp.float32),
            pltpu.VMEM((NB, count, bs), jnp.bfloat16),
        ],
        compiler_params=pltpu.CompilerParams(vmem_limit_bytes=VMEM_LIMIT),
        cost_estimate=NO_COST,
        name=name,
    )(values, *args)


def after(array, *done):
    return lax.optimization_barrier((array, *done))[0]


def body(rhs, diag_inv, panel, offdiag, known, row_index):
    plan = Plan(lax.axis_size("row"), lax.axis_size("col"))
    core = lax.rem(lax.axis_index("row"), 2)

    folded, known = fold_panel(panel, diag_inv, known, plan.slots, plan.cols)
    line = [folded] + [across_z(folded, plan, m) for m in range(1, plan.zs)]
    known_all = lax.all_to_all(known, "col", 0, 0)
    sums = segment_sums(offdiag, row_index, known.shape[0] * known.shape[1])
    within, cross = pack(plan, [after(piece, sums, known_all) for piece in line])

    got = direct(within, plan)

    keep, give = local_update(known_all, after(sums, cross), rhs, diag_inv)
    total = keep + other_core(give, plan).astype(jnp.float32)
    sent = total.astype(jnp.bfloat16)
    for m in range(1, plan.zs // 2):
        total = total + across_z(sent, plan, m).astype(jnp.float32)
    sent = total.astype(jnp.bfloat16)
    total = total + across_z(sent, plan, plan.zs - 1).astype(jnp.float32)
    cross = jnp.stack([cross, other_core(cross, plan)])
    upper = after(total[plan.upper].astype(jnp.bfloat16), cross, got[1])
    values = jnp.stack(direct(upper, plan))

    split = plan.counts[0]
    early, late = jnp.stack(got[:-1]), got[-1][None]
    high = [jnp.concatenate([early[:, :split], late[:, :split]])]
    high.append(
        jnp.concatenate([other_core(piece[:, :split], plan) for piece in (early, late)])
    )
    high = jnp.stack(high)
    low = jnp.concatenate([early[:, split:], late[:, split:]])
    sizes = (NB // 2, plan.lower.stop)
    solved, lower = call_half(
        upper_kernel, plan, "upper_half", sizes, values, total[plan.lower], high, cross
    )
    values = jnp.stack(direct(lower, plan))
    low = after(low, solved)
    low = jnp.stack([low, other_core(low, plan)])
    (mine,) = call_half(
        lower_kernel, plan, "lower_half", (NB // plan.cols,), values, solved, low
    )
    mine, theirs = out_of_solvers(mine, plan)
    return jnp.concatenate(
        [jnp.where(core == 0, mine, theirs), jnp.where(core == 0, theirs, mine)], axis=1
    )


def solution(mesh):
    placed = (
        P("col", None, None),
        P("col", None, None),
        P("row", "col", None, None),
        P("row", "col", None, None),
        P(("row", "col"), None, None),
        P("row"),
    )
    return jax.shard_map(
        body, mesh=mesh, in_specs=placed, out_specs=P("col", None, None), check_vma=False
    )
```

```python
import functools

import jax
import jax.numpy as jnp
from jax import lax
from jax.experimental import pallas as pl
from jax.experimental.pallas import tpu as pltpu
from jax.sharding import PartitionSpec as P

NB = 16
AXES = ("row", "col")
VMEM_LIMIT = 16 * 1024 * 1024
HIGHEST = lax.Precision.HIGHEST


class Plan:
    def __init__(self, rows, cols):
        self.rows, self.cols, self.zs = rows, cols, rows // 2
        self.slots = [
            (a, b)
            for a in reversed(range(NB // rows))
            for b in reversed(range(NB // cols))
            if a * rows + rows - 1 > b * cols
        ]
        half = NB // 2
        self.high, self.low, self.cross = {}, {}, {}
        for core in range(2):
            for c in range(cols):
                below = [
                    (r, at, a * rows + r, b * cols + c)
                    for r in range(core, rows, 2)
                    for at, (a, b) in enumerate(self.slots)
                    if a * rows + r > b * cols + c
                ]
                self.high[core, c] = [t[:2] for t in below if t[3] >= half]
                self.low[core, c] = [t[:2] for t in below if t[2] < half]
                self.cross[core, c] = [t[:2] for t in below if t[2] >= half > t[3]]
        self.lists = (self.high, self.low, self.cross)
        self.counts = [max(map(len, lists.values())) for lists in self.lists]
        self.upper = slice(half // cols, NB // cols)
        self.lower = slice(0, -(-half // cols))
        self.solvers = sorted({max(self.zs // 2 - 1, 0), self.zs // 2})
        self.arrival = [self.zs - 1, *range(1, self.zs - 1), 0]


def send(array, plan, pairs):
    flat = [(r * plan.cols + c, to_r * plan.cols + to_c) for (r, c), (to_r, to_c) in pairs]
    return lax.ppermute(array, AXES, flat)


def across_z(array, plan, flip):
    to = {z ^ flip: z for z in plan.solvers}
    free = [z for z in range(plan.zs) if z not in to.values()]
    for z in range(plan.zs):
        if z not in to:
            to[z] = min(free, key=lambda other: abs(other - z))
            free.remove(to[z])
    pairs = [
        ((2 * z + core, c), (2 * to[z] + core, c))
        for z in range(plan.zs)
        for core in range(2)
        for c in range(plan.cols)
    ]
    return send(array, plan, pairs)


def out_of_solvers(array, plan):
    low, high = plan.solvers[0], plan.solvers[-1]
    z = lax.axis_index("row") // 2
    own, other = array, other_core(array, plan)
    for step in range(1, plan.zs // 2):
        to = {low: low - step, high: high + step, low - step: low, high + step: high}
        outer = jnp.logical_or(z == low - step, z == high + step)
        got = []
        for cross in range(2):
            pairs = [
                ((2 * a + core, c), (2 * to.get(a, a) + (core ^ cross), c))
                for a in range(plan.zs)
                for core in range(2)
                for c in range(plan.cols)
            ]
            got.append(send(array, plan, pairs))
        own, other = jnp.where(outer, got[0], own), jnp.where(outer, got[1], other)
    return own, other


def across_col(array, plan, flip):
    pairs = [((r, c), (r, c ^ flip)) for r in range(plan.rows) for c in range(plan.cols)]
    return send(array, plan, pairs)


def other_core(array, plan):
    pairs = [((r, c), (r ^ 1, c)) for r in range(plan.rows) for c in range(plan.cols)]
    return send(array, plan, pairs)


def direct(array, plan):
    return [array] + [across_col(array, plan, m) for m in range(1, plan.cols)]


NO_COST = pl.CostEstimate(flops=0, bytes_accessed=0, transcendentals=0)


def fold_kernel(slots, panel_hbm, inverse_hbm, known_hbm, out_ref, known_ref, panel_ref, inverse_ref, sems):
    copies = [
        pltpu.make_async_copy(inverse_hbm, inverse_ref, sems.at[0]),
        pltpu.make_async_copy(panel_hbm, panel_ref, sems.at[1]),
    ]
    copies += [
        pltpu.make_async_copy(known_hbm, known_ref.at[c], sems.at[2 + c])
        for c in range(known_ref.shape[0])
    ]
    for copy in copies:
        copy.start()
    for copy in copies:
        copy.wait()
    for at, (a, b) in enumerate(slots):
        inverse = inverse_ref[b]
        high = inverse.astype(jnp.bfloat16)
        low = (inverse - high.astype(jnp.float32)).astype(jnp.bfloat16)
        tile = panel_ref[a, b]
        out_ref[at] = (
            jnp.dot(tile, high, preferred_element_type=jnp.float32)
            + jnp.dot(tile, low, preferred_element_type=jnp.float32)
        ).astype(jnp.bfloat16)


def fold_panel(panel, inverse, known, slots, cols):
    bs = panel.shape[-1]
    return pl.pallas_call(
        functools.partial(fold_kernel, slots),
        in_specs=[pl.BlockSpec(memory_space=pltpu.HBM)] * 3,
        out_shape=(
            jax.ShapeDtypeStruct((len(slots), bs, bs), jnp.bfloat16),
            jax.ShapeDtypeStruct((cols, *known.shape), known.dtype),
        ),
        scratch_shapes=[
            pltpu.VMEM(panel.shape, panel.dtype),
            pltpu.VMEM(inverse.shape, inverse.dtype),
            pltpu.SemaphoreType.DMA((2 + cols,)),
        ],
        compiler_params=pltpu.CompilerParams(vmem_limit_bytes=62 * 1024 * 1024),
        cost_estimate=NO_COST,
        name="fold_panel",
    )(panel, inverse, known)


def segment_kernel(chunk, index_ref, tiles_hbm, out_ref, tiles, sums, sems):
    copies = [
        pltpu.make_async_copy(
            tiles_hbm.at[pl.ds(i * chunk, chunk)], tiles.at[pl.ds(i * chunk, chunk)], sems.at[i]
        )
        for i in range(tiles.shape[0] // chunk)
    ]
    for copy in copies:
        copy.start()
    sums[...] = jnp.zeros_like(sums)
    for i, copy in enumerate(copies):
        copy.wait()

        def add(p, carry):
            sums[index_ref[p]] += tiles[p].astype(jnp.float32)
            return carry

        lax.fori_loop(i * chunk, (i + 1) * chunk, add, 0)
    out_ref[...] = sums[...].astype(jnp.bfloat16)


def segment_sums(offdiag, row_index, segments):
    tiles, blocks, bs, _ = offdiag.shape
    chunk = 4
    return pl.pallas_call(
        functools.partial(segment_kernel, chunk),
        in_specs=[pl.BlockSpec(memory_space=pltpu.SMEM), pl.BlockSpec(memory_space=pltpu.HBM)],
        out_shape=jax.ShapeDtypeStruct((segments, blocks, bs, bs), jnp.bfloat16),
        scratch_shapes=[
            pltpu.VMEM(offdiag.shape, offdiag.dtype),
            pltpu.VMEM((segments, blocks, bs, bs), jnp.float32),
            pltpu.SemaphoreType.DMA((tiles // chunk,)),
        ],
        compiler_params=pltpu.CompilerParams(vmem_limit_bytes=52 * 1024 * 1024),
        cost_estimate=pl.CostEstimate(
            flops=offdiag.size, bytes_accessed=2 * offdiag.size, transcendentals=0
        ),
        name="segment_sums",
    )(row_index, offdiag)


def update_kernel(known_ref, sums_ref, rhs_ref, inverse_ref, keep_ref, give_ref, whole):
    blocks, count, bs = rhs_ref.shape
    cols, per = known_ref.shape[:2]
    row_id = lax.axis_index("row")
    off = [jnp.zeros((count, bs), jnp.float32)] * blocks
    for c in range(cols):
        for i in range(per):
            for b in range(blocks):
                off[b] += jnp.dot(
                    known_ref[c, i], sums_ref[c * per + i, b], preferred_element_type=jnp.float32
                )
    adds = (row_id == 0).astype(jnp.float32)
    for b in range(blocks):
        total = rhs_ref[b] * adds - off[b]
        whole[b] = jnp.dot(
            total, inverse_ref[b], precision=HIGHEST, preferred_element_type=jnp.float32
        )
    half = count // 2
    core = lax.rem(row_id, 2)
    keep = pl.ds(pl.multiple_of(core * half, half), half)
    give = pl.ds(pl.multiple_of((1 - core) * half, half), half)
    keep_ref[...] = whole[:, keep, :]
    give_ref[...] = whole[:, give, :].astype(jnp.bfloat16)


def local_update(known, sums, rhs, inverse):
    blocks, count, bs = rhs.shape
    half = (blocks, count // 2, bs)
    return pl.pallas_call(
        update_kernel,
        out_shape=(
            jax.ShapeDtypeStruct(half, jnp.float32),
            jax.ShapeDtypeStruct(half, jnp.bfloat16),
        ),
        scratch_shapes=[pltpu.VMEM(rhs.shape, jnp.float32)],
        compiler_params=pltpu.CompilerParams(vmem_limit_bytes=VMEM_LIMIT),
        cost_estimate=NO_COST,
        name="local_update",
    )(known, sums, rhs, inverse)


def pack_kernel(plan, *refs):
    line_refs = [refs[plan.arrival.index(step)] for step in range(plan.zs)]
    row_id, col_id = lax.axis_index("row"), lax.axis_index("col")
    core, z = lax.rem(row_id, 2), row_id // 2
    within_ref, cross_ref = refs[plan.zs :]
    for which, (lists, count) in enumerate(zip(plan.lists, plan.counts)):
        out_ref = cross_ref if which == 2 else within_ref
        first = plan.counts[0] if which == 1 else 0
        for i in range(count):
            back, at = jnp.int32(0), jnp.int32(0)
            for (side, c), found in lists.items():
                if i < len(found):
                    mine = jnp.logical_and(col_id == c, core == side)
                    back = jnp.where(mine, lax.bitwise_xor(z, found[i][0] // 2), back)
                    at = jnp.where(mine, found[i][1], at)
            for step, line_ref in enumerate(line_refs):

                @pl.when(back == step)
                def _():
                    out_ref[first + i] = line_ref[at]


def pack(plan, line):
    bs = line[0].shape[-1]
    return pl.pallas_call(
        functools.partial(pack_kernel, plan),
        out_shape=[
            jax.ShapeDtypeStruct((count, bs, bs), jnp.bfloat16)
            for count in (sum(plan.counts[:2]), plan.counts[2])
        ],
        compiler_params=pltpu.CompilerParams(vmem_limit_bytes=VMEM_LIMIT),
        cost_estimate=NO_COST,
        name="pack",
    )(*[line[step] for step in plan.arrival])


def solve(plan, value_ref, tiles_ref, values, solved, first):
    rows, cols, half = plan.rows, plan.cols, NB // 2
    core, col_id = lax.rem(lax.axis_index("row"), 2), lax.axis_index("col")
    for step in range(cols):
        owner = lax.bitwise_xor(col_id, step)
        for b in range(value_ref.shape[1]):
            values[b * cols + owner] = value_ref[step, b].astype(jnp.float32)

    def tile(j, k):
        r, c = j % rows, k % cols
        lists = plan.high if first else plan.low
        at = lists[r % 2, c].index((r, plan.slots.index((j // rows, k // cols))))
        return tiles_ref[lax.bitwise_xor(core, r % 2), lax.bitwise_xor(col_id, c), at]

    skip = first // cols * cols
    sums = [values[first - skip + i] for i in range(half)]
    for i in reversed(range(half)):
        block = sums[i].astype(jnp.bfloat16)
        solved[first + i] = block
        for m in reversed(range(i)):
            sums[m] = sums[m] - jnp.dot(
                block, tile(first + i, first + m), preferred_element_type=jnp.float32
            )


def upper_kernel(plan, value_ref, own_ref, tiles_ref, cross_ref, out_ref, lower_ref, values, solved):
    rows, half = plan.rows, NB // 2
    core = lax.rem(lax.axis_index("row"), 2)
    solve(plan, value_ref, tiles_ref, values, solved, half)
    out_ref[...] = solved[pl.ds(half, half)]
    for b in range(own_ref.shape[0]):
        total = own_ref[b]
        for j in range(half, NB):
            r = j % rows
            at = plan.cross[r % 2, 0].index((r, plan.slots.index((j // rows, b))))
            tile = cross_ref[lax.bitwise_xor(core, r % 2), at]
            total = total - jnp.dot(solved[j], tile, preferred_element_type=jnp.float32)
        lower_ref[b] = total.astype(jnp.bfloat16)


def lower_kernel(plan, value_ref, upper_ref, tiles_ref, out_ref, values, solved):
    half, col_id = NB // 2, lax.axis_index("col")
    solved[pl.ds(half, half)] = upper_ref[...]
    solve(plan, value_ref, tiles_ref, values, solved, 0)
    for b in range(out_ref.shape[0]):
        out_ref[b] = solved[b * plan.cols + col_id]


def call_half(kernel, plan, name, out_shape, values, *args):
    _, blocks, count, bs = values.shape
    return pl.pallas_call(
        functools.partial(kernel, plan),
        out_shape=[jax.ShapeDtypeStruct((n, count, bs), jnp.bfloat16) for n in out_shape],
        scratch_shapes=[
            pltpu.VMEM((blocks * plan.cols, count, bs), jnp.float32),
            pltpu.VMEM((NB, count, bs), jnp.bfloat16),
        ],
        compiler_params=pltpu.CompilerParams(vmem_limit_bytes=VMEM_LIMIT),
        cost_estimate=NO_COST,
        name=name,
    )(values, *args)


def after(array, *done):
    return lax.optimization_barrier((array, *done))[0]


def body(rhs, diag_inv, panel, offdiag, known, row_index):
    plan = Plan(lax.axis_size("row"), lax.axis_size("col"))
    core = lax.rem(lax.axis_index("row"), 2)

    folded, known = fold_panel(panel, diag_inv, known, plan.slots, plan.cols)
    line = [folded] + [across_z(folded, plan, m) for m in range(1, plan.zs)]
    known_all = lax.all_to_all(known, "col", 0, 0)
    sums = segment_sums(offdiag, row_index, known.shape[0] * known.shape[1])
    within, cross = pack(plan, [after(piece, known_all) for piece in line])

    got = direct(within, plan)

    keep, give = local_update(known_all, after(sums, cross), rhs, diag_inv)
    total = keep + other_core(give, plan).astype(jnp.float32)
    sent = total.astype(jnp.bfloat16)
    for m in range(1, plan.zs // 2):
        total = total + across_z(sent, plan, m).astype(jnp.float32)
    sent = total.astype(jnp.bfloat16)
    total = total + across_z(sent, plan, plan.zs - 1).astype(jnp.float32)
    cross = jnp.stack([cross, other_core(cross, plan)])
    upper = after(total[plan.upper].astype(jnp.bfloat16), cross, got[1])
    values = jnp.stack(direct(upper, plan))

    split = plan.counts[0]
    early, late = jnp.stack(got[:-1]), got[-1][None]
    high = [jnp.concatenate([early[:, :split], late[:, :split]])]
    high.append(
        jnp.concatenate([other_core(piece[:, :split], plan) for piece in (early, late)])
    )
    high = jnp.stack(high)
    low = jnp.concatenate([early[:, split:], late[:, split:]])
    sizes = (NB // 2, plan.lower.stop)
    solved, lower = call_half(
        upper_kernel, plan, "upper_half", sizes, values, total[plan.lower], high, cross
    )
    values = jnp.stack(direct(lower, plan))
    low = after(low, solved)
    low = jnp.stack([low, other_core(low, plan)])
    (mine,) = call_half(
        lower_kernel, plan, "lower_half", (NB // plan.cols,), values, solved, low
    )
    mine, theirs = out_of_solvers(mine, plan)
    return jnp.concatenate(
        [jnp.where(core == 0, mine, theirs), jnp.where(core == 0, theirs, mine)], axis=1
    )


def solution(mesh):
    placed = (
        P("col", None, None),
        P("col", None, None),
        P("row", "col", None, None),
        P("row", "col", None, None),
        P(("row", "col"), None, None),
        P("row"),
    )
    return jax.shard_map(
        body, mesh=mesh, in_specs=placed, out_specs=P("col", None, None), check_vma=False
    )
```
